256 devices in a mesh: cache: 32 (over y_lo, z, core), heads: 8 (over x, y_hi).
Axes of the slice: x: 4, y: 4 (y_hi: 2, y_lo: 2; y = y_hi * 2 + y_lo), z: 8, core: 2. Of those that a mesh axis runs over, the one named last changes fastest.
Arguments:
- queries: bfloat16 [4096, 4096], P('cache', 'heads'), may hold values from -10 to 10
- cache_keys: bfloat16 [49152, 1024], P('cache', 'heads'), may hold values from -6 to 6
- cache_values: bfloat16 [49152, 1024], P('cache', 'heads'), may hold values from -6 to 6
- suffix_keys: bfloat16 [4096, 1024], P('cache', 'heads'), may hold values from -8 to 8
- suffix_values: bfloat16 [4096, 1024], P('cache', 'heads'), may hold values from -6 to 6
- out_weight: bfloat16 [4096, 8192], P('heads'), may hold values from -0.09375 to 0.09375
- ancestor_mask: int32 [64, 384], P(None, 'cache'), may hold values from 0 to 1, as said below
- leaf_node: int32 [32], P('cache'), may hold values from 0 to 63
- suffix_len: int32 [32], P('cache'), may hold values from 2 to 128, as said below
Outputs:
- mixed: bfloat16 [4096, 8192], P('cache', 'heads')
The draws below stay inside these ranges and needn't reach their ends.
Inputs may be any that keep to these rules, and one draw needn't show every extreme that they name: ancestor_mask[n, c] is 1 exactly when the tree node that owns cache block c is n or an ancestor of n; node 0 is the root. `suffix_len`: some block has all 128 suffix tokens live.
All inputs are finite; a program needn't handle non-finite values.
Results may differ from the reference program's by a relative error of at most 0.011.
Values may be sent and summed in bfloat16 or wider, within the bound.
No kernel may reach another device: no remote copies, remote signals or barrier semaphores. Data moves between devices by JAX's collectives and lax.ppermute only.
A program may use at most 128 MiB of HBM per device.

```python
import math
import jax
import jax.numpy as jnp
from jax import lax

D = 8192
HD = 128
QPG = 4
BLK = 128
NODES = 64
KVH = 8
QBLOCKS = 32
TOKENS = 4096
CBLOCKS = 384
CTOK = 49152


def draw_queries(key, part):
    key = jax.random.fold_in(key, 1)
    base_key = jax.random.fold_in(key, 0)
    values = jnp.clip(2.0 * jax.random.normal(base_key, (TOKENS, KVH * QPG * HD), jnp.float32), -10.0, 10.0)
    return values.astype(jnp.bfloat16)


def draw_suffix_keys(key, part):
    key = jax.random.fold_in(key, 2)
    base_key = jax.random.fold_in(key, 0)
    values = jnp.clip(1.5 * jax.random.normal(base_key, (TOKENS, KVH * HD), jnp.float32), -8.0, 8.0)
    return values.astype(jnp.bfloat16)


def draw_ancestor_mask(key, part):
    key = jax.random.fold_in(key, 3)
    parent_key, owner_key = jax.random.split(key)
    raw_draw = jax.random.randint(parent_key, (NODES,), 0, 1 << 30)
    parents = raw_draw % jnp.maximum(jnp.arange(NODES, dtype=jnp.int32), 1)
    owners = jax.random.randint(owner_key, (CBLOCKS,), 0, NODES)

    def link(member, lineage):
        family = lineage[parents[member]].at[member].set(1)
        return lineage.at[member].set(family)
    lineage = lax.fori_loop(1, NODES, link, jnp.eye(NODES, dtype=jnp.int32))
    return jnp.take(lineage, owners, axis=1).astype(jnp.int32)


def draw_suffix_len(key, part):
    key = jax.random.fold_in(key, 4)
    length_key, spot_key = jax.random.split(key)
    lengths = jax.random.randint(length_key, (QBLOCKS,), 2, BLK + 1)
    spot_block = jax.random.randint(spot_key, (), 0, QBLOCKS)
    return jnp.where(jnp.arange(QBLOCKS) == spot_block, BLK, lengths).astype(jnp.int32)


def place_ends(entries, key, low, top_value):
    shape = entries.shape
    index_at = [jax.random.randint(jax.random.fold_in(key, axis), (), 0, shape[axis]) for axis in range(len(shape))]
    entries = entries.at[tuple(index_at)].set(low)
    longest = shape.index(max(shape))
    index_at[longest] = (index_at[longest] + 1) % shape[longest]
    return entries.at[tuple(index_at)].set(top_value)


def block_levels(stream_key, extent, shards, smallest, top_value):
    level, own = 1.0, jax.random.fold_in(stream_key, 6)
    for dim, parts in shards:
        heights = jnp.exp(jax.random.uniform(jax.random.fold_in(own, dim), (parts,), jnp.float32, smallest / len(shards), top_value / len(shards)))
        level = level * jnp.repeat(heights, extent[dim] // parts).reshape([-1 if axis == dim else 1 for axis in range(len(extent))])
    return level


def bell_draw(key, shape, width, most, cuts=(), held_as=jnp.bfloat16):
    result = width * jax.random.normal(key, shape, jnp.float32)
    if cuts:
        result = result * block_levels(key, shape, cuts, -0.22, 0.18)
    return jnp.clip(result, -most, most).astype(held_as)


def setup_inputs(seed: int = 0) -> dict:
    seeds = jax.random.split(jax.random.key(seed), 10)
    queries = draw_queries(jax.random.fold_in(seeds[9], 71), 0)
    cache_keys = bell_draw(seeds[1], (CTOK, KVH * HD), 1.0, 6.0, ((0, 32), (1, 8)))
    cache_values = bell_draw(seeds[2], (CTOK, KVH * HD), 1.0, 6.0, ((0, 32), (1, 8)))
    suffix_keys = draw_suffix_keys(jax.random.fold_in(seeds[9], 71), 0)
    suffix_values = bell_draw(seeds[4], (TOKENS, KVH * HD), 1.0, 6.0, ((0, 32), (1, 8)))
    out_weight = bell_draw(seeds[5], (KVH * QPG * HD, D), (KVH * QPG * HD) ** -0.5, 0.09375, ((0, 8),))
    ancestor_mask = draw_ancestor_mask(jax.random.fold_in(seeds[9], 71), 0)
    leaf_node = place_ends(jax.random.randint(seeds[7], (QBLOCKS,), 0, NODES), jax.random.fold_in(seeds[7], 1), 0, NODES - 1).astype(jnp.int32)
    suffix_len = draw_suffix_len(jax.random.fold_in(seeds[9], 71), 0)
    return dict(queries=queries, cache_keys=cache_keys, cache_values=cache_values, suffix_keys=suffix_keys, suffix_values=suffix_values, out_weight=out_weight, ancestor_mask=ancestor_mask, leaf_node=leaf_node, suffix_len=suffix_len)


def absorb(running, query_rows, allowed, key_rows, value_rows, score_scale):
    maxima, totals, summed = running
    scores = lax.dot_general(query_rows, key_rows, (((1,), (1,)), ((), ())), preferred_element_type=jnp.float32) * score_scale
    scores = jnp.where(allowed, scores, -jnp.inf)
    updated = jnp.maximum(maxima, lax.optimization_barrier(jnp.max(scores, axis=1)))
    steady = jnp.where(jnp.isfinite(updated), updated, 0.0)
    weights = jnp.exp(scores - steady[:, None])
    rescale = jnp.exp(maxima - steady)
    totals = totals * rescale + lax.optimization_barrier(jnp.sum(weights, axis=1))
    summed = summed * rescale[:, None] + jnp.dot(weights.astype(jnp.bfloat16), value_rows, preferred_element_type=jnp.float32)
    return (updated, totals, summed)

def own_suffix(query_rows, key_rows, value_rows, lengths, heads_here, block_len, score_scale):
    row_count = query_rows.shape[0]
    row_tok = jnp.arange(row_count, dtype=jnp.int32) // heads_here
    col_tok = jnp.arange(key_rows.shape[0], dtype=jnp.int32)
    same_block = row_tok[:, None] // block_len == col_tok[None, :] // block_len
    causal = col_tok[None, :] % block_len <= row_tok[:, None] % block_len
    live_keys = col_tok % block_len < jnp.repeat(lengths, block_len)
    allowed = same_block & causal & live_keys[None, :]
    initial = (jnp.full((row_count,), -jnp.inf, jnp.float32), jnp.zeros((row_count,), jnp.float32), jnp.zeros((row_count, key_rows.shape[1]), jnp.float32))
    return absorb(initial, query_rows, allowed, key_rows, value_rows, score_scale)

def reference(queries, cache_keys, cache_values, suffix_keys, suffix_values, out_weight, ancestor_mask, leaf_node, suffix_len):
    score_scale = 1.0 / math.sqrt(HD)
    query_blocks = queries.reshape(QBLOCKS, BLK, KVH, QPG, HD).transpose(0, 2, 1, 3, 4).reshape(QBLOCKS, KVH, BLK * QPG, HD)
    suffix_key_blocks = suffix_keys.reshape(QBLOCKS, BLK, KVH, HD).transpose(0, 2, 1, 3)
    suffix_value_blocks = suffix_values.reshape(QBLOCKS, BLK, KVH, HD).transpose(0, 2, 1, 3)
    cache_key_blocks = cache_keys.reshape(CBLOCKS, BLK, KVH, HD).transpose(0, 2, 1, 3)
    cache_value_blocks = cache_values.reshape(CBLOCKS, BLK, KVH, HD).transpose(0, 2, 1, 3)
    everywhere = jnp.ones((BLK * QPG, BLK), dtype=bool)

    def one_block(block_item):
        query_rows, key_rows, value_rows, leaf_id, length = block_item

        def opening(head_rows, head_keys, head_values):
            return own_suffix(head_rows, head_keys, head_values, length[None], QPG, BLK, score_scale)
        running = jax.vmap(opening)(query_rows, key_rows, value_rows)
        visible = ancestor_mask[leaf_id]

        def absorb_head(maxima, totals, summed, head_rows, head_keys, head_values):
            return absorb((maxima, totals, summed), head_rows, everywhere, head_keys, head_values, score_scale)

        def absorb_block(running, cache_block):
            block_keys = lax.dynamic_index_in_dim(cache_key_blocks, cache_block, 0, keepdims=False)
            block_values = lax.dynamic_index_in_dim(cache_value_blocks, cache_block, 0, keepdims=False)

            def taken(current):
                return jax.vmap(absorb_head)(current[0], current[1], current[2], query_rows, block_keys, block_values)

            def skipped(current):
                return current
            return (lax.cond(visible[cache_block] > 0, taken, skipped, running), None)
        running, ignored = lax.scan(absorb_block, running, jnp.arange(CBLOCKS, dtype=jnp.int32))
        return (running[2] / running[1][..., None]).astype(jnp.bfloat16)
    attended = lax.map(one_block, (query_blocks, suffix_key_blocks, suffix_value_blocks, leaf_node, suffix_len))
    attended = attended.reshape(QBLOCKS, KVH, BLK, QPG, HD).transpose(0, 2, 1, 3, 4).reshape(TOKENS, KVH * QPG * HD)
    return jnp.dot(attended, out_weight, preferred_element_type=jnp.float32).astype(jnp.bfloat16)
```

```python
import math

import jax
import jax.numpy as jnp
from jax import lax
from jax.experimental import pallas as pl
from jax.experimental.pallas import tpu as pltpu
from jax.sharding import PartitionSpec as P

BF16 = jnp.bfloat16
F32 = jnp.float32
NY, NZ, NC = 2, 8, 2
NX, NW = 4, 2
HD = 128
BLK = 128
QPG = 4
ROWS = QPG * BLK
EMPTY = -1e30
SCALE2 = math.log2(math.e) / math.sqrt(HD)
OFFSETS = (0, 1, -1, 2, -2, 3, -3, 4)
NEAR = 5
RELATIVE = tuple((dx, dw) for dx in (0, 2, 1, 3) for dw in (0, 1))
PAYLOAD = BLK + 16
PER_SOURCE = 12
KEYS_AT, VALUES_AT, MASK_AT = 0, PER_SOURCE * BLK, 2 * PER_SOURCE * BLK
SOURCE = MASK_AT + 16


def cache_step(x, dy, dz, dc):
    pairs = []
    for y in range(NY):
        for z in range(NZ):
            for c in range(NC):
                there = (((y + dy) % NY) * NZ + (z + dz) % NZ) * NC + (c + dc) % NC
                pairs.append(((y * NZ + z) * NC + c, there))
    return lax.ppermute(x, "cache", pairs)


def heads_step(x, dx, dw):
    pairs = []
    for a in range(NX):
        for w in range(NW):
            pairs.append((a * NW + w, ((a + dx) % NX) * NW + (w + dw) % NW))
    return lax.ppermute(x, "heads", pairs)


def z_ways(x, even, odd):
    pairs = []
    for y in range(NY):
        for z in range(NZ):
            for c in range(NC):
                there = (y * NZ + (z + (odd if z % 2 else even)) % NZ) * NC + c
                pairs.append(((y * NZ + z) * NC + c, there))
    return lax.ppermute(x, "cache", pairs)


def scores_of(keys, rows):
    return lax.dot_general(keys, rows, (((1,), (1,)), ((), ())), preferred_element_type=F32)


def weighted(values, weights):
    return lax.dot_general(
        values, weights.astype(BF16), (((0,), (0,)), ((), ())), preferred_element_type=F32
    )


def softmax_part(scores):
    peak = jnp.max(scores, axis=0, keepdims=True)
    weights = jnp.exp2((scores - peak) * SCALE2)
    return peak, jnp.sum(weights, axis=0, keepdims=True), weights


def fetch(packed, sources, qbuf, lbuf, sbuf, qsem, ssem):
    copies = []
    for b, ref in enumerate(packed):
        for h in range(QPG):
            copies.append(
                pltpu.make_async_copy(
                    ref.at[pl.ds(0, BLK), pl.ds(h * HD, HD)],
                    qbuf.at[b, pl.ds(h * BLK, BLK), :],
                    qsem.at[b * (QPG + 1) + h],
                )
            )
        copies.append(
            pltpu.make_async_copy(
                ref.at[pl.ds(BLK, 16), pl.ds(0, HD)], lbuf.at[b], qsem.at[b * (QPG + 1) + QPG]
            )
        )
    for s, ref in enumerate(sources):
        copies.append(pltpu.make_async_copy(ref, sbuf.at[s], ssem.at[s]))
    return copies


def list_items(wanted, lbuf, sbuf, vis_v, vis_s, todo, dummy, vsem):
    blocks = sorted({b for b, _ in wanted})
    leaf = jnp.concatenate([lbuf[b].astype(F32)[0:1, :] for b in blocks], axis=0)
    node_at = lax.broadcasted_iota(jnp.int32, leaf.shape, 1).astype(F32)
    chosen = jnp.where(node_at == leaf, 1.0, 0.0).astype(BF16)
    for s in sorted({s for _, s in wanted}):
        seen = scores_of(chosen, sbuf[s, MASK_AT:SOURCE, :])
        vis_v[8 * s : 8 * s + len(blocks), 0:16] = seen.astype(jnp.int32)
    copy = pltpu.make_async_copy(vis_v, vis_s, vsem)
    copy.start()
    copy.wait()
    count = jnp.int32(0)
    for b, s in wanted:
        for c in range(PER_SOURCE):
            todo[count] = b * 64 + s * 16 + c
            count = count + vis_s[8 * s + b, c]
    todo[count] = dummy * 64
    return count


def work(count, todo, nq, qbuf, sbuf, state):
    def part(item):
        b = lax.shift_right_logical(item, 6)
        s = lax.bitwise_and(lax.shift_right_logical(item, 4), 3)
        row = pl.multiple_of(lax.bitwise_and(item, 15) * BLK, BLK)
        keys = sbuf[s, pl.ds(row, BLK), :]
        values = sbuf[s, pl.ds(VALUES_AT + row, BLK), :]
        peak, total, weights = softmax_part(scores_of(keys, qbuf[jnp.minimum(b, nq - 1)]))
        return b, peak, total, weighted(values, weights)

    def pair(i, carry):
        first = part(todo[2 * i])
        second = part(todo[2 * i + 1])
        merge(state, *first)
        merge(state, *second)
        return carry

    lax.fori_loop(0, lax.shift_right_logical(count + 1, 1), pair, 0)


def merge(state, b, peak, total, summed):
    peaks, totals, sums = state
    before = peaks[b]
    after = jnp.maximum(before, peak)
    keep = jnp.exp2((before - after) * SCALE2)
    take = jnp.exp2((peak - after) * SCALE2)
    peaks[b] = after
    totals[b] = totals[b] * keep + total * take
    sums[b] = sums[b] * keep + summed * take


def first_kernel(length, *refs):
    packed, sources = refs[0:NEAR], refs[NEAR : NEAR + 2]
    suffix_k, suffix_v = refs[NEAR + 2 : NEAR + 4]
    state = refs[NEAR + 4 : NEAR + 7]
    todo, vis_s, vis_v, qbuf, lbuf, sbuf, qsem, ssem, vsem = refs[NEAR + 7 :]
    copies = fetch(packed, sources, qbuf, lbuf, sbuf, qsem, ssem)
    for copy in copies:
        copy.start()
    peaks, totals, sums = state
    peaks[...] = jnp.full(peaks.shape, EMPTY, F32)
    totals[...] = jnp.zeros(totals.shape, F32)
    sums[...] = jnp.zeros(sums.shape, F32)
    for copy in copies:
        copy.wait()
    wanted = [(b, s) for b in range(NEAR) for s in range(2)]
    count = list_items(wanted, lbuf, sbuf, vis_v, vis_s, todo, NEAR, vsem)
    work(count, todo, NEAR, qbuf, sbuf, state)
    key_at = lax.broadcasted_iota(jnp.int32, (BLK, ROWS), 0)
    row_at = lax.bitwise_and(lax.broadcasted_iota(jnp.int32, (BLK, ROWS), 1), BLK - 1)
    scores = scores_of(suffix_k[...], qbuf[0])
    scores = jnp.where((key_at <= row_at) & (key_at < length[0]), scores, EMPTY)
    peak, total, weights = softmax_part(scores)
    merge(state, 0, peak, total, weighted(suffix_v[...], weights))


def lse_rows(lse):
    high = lse.astype(BF16).astype(F32)
    middle = (lse - high).astype(BF16).astype(F32)
    low = lse - high - middle
    at = lax.broadcasted_iota(jnp.int32, (16, ROWS), 0)
    return jnp.where(at == 0, high, jnp.where(at == 1, middle, low)).astype(BF16)


def lse_of(rows):
    pieces = rows.astype(F32)
    return pieces[0:1] + pieces[1:2] + pieces[2:3]


def second_kernel(*refs):
    nq = len(OFFSETS)
    packed, sources, known = refs[0:nq], refs[nq : nq + 4], refs[nq + 4 : nq + 7]
    own_out, own_lse = refs[nq + 7 : nq + 9]
    payloads = refs[nq + 9 : 2 * nq + 8]
    todo, vis_s, vis_v, qbuf, lbuf, sbuf, peaks, totals, sums, qsem, ssem, vsem, ksem = refs[
        2 * nq + 8 :
    ]
    state = (peaks, totals, sums)
    copies = fetch(packed, sources, qbuf, lbuf, sbuf, qsem, ssem)
    for i in range(3):
        copies.append(
            pltpu.make_async_copy(
                known[i].at[pl.ds(0, NEAR)], state[i].at[pl.ds(0, NEAR)], ksem.at[i]
            )
        )
    for copy in copies:
        copy.start()
    for b in range(NEAR, nq + 1):
        peaks[b] = jnp.full((1, ROWS), EMPTY, F32)
        totals[b] = jnp.zeros((1, ROWS), F32)
        sums[b] = jnp.zeros((HD, ROWS), F32)
    for copy in copies:
        copy.wait()
    wanted = [(b, s) for b in range(NEAR, nq) for s in range(4)]
    wanted += [(b, s) for b in range(NEAR) for s in (2, 3)]
    count = list_items(wanted, lbuf, sbuf, vis_v, vis_s, todo, nq, vsem)
    work(count, todo, nq, qbuf, sbuf, state)
    for b in range(nq):
        total = totals[b]
        seen = total > 0.0
        safe = jnp.where(seen, total, 1.0)
        lse = jnp.where(seen, peaks[b] * SCALE2 + jnp.log2(safe), EMPTY)
        out = sums[b] * (1.0 / safe)
        if b == 0:
            own_out[...] = out
            own_lse[...] = jnp.broadcast_to(lse, own_lse.shape)
        else:
            payloads[b - 1][0:BLK, :] = out.astype(BF16)
            payloads[b - 1][BLK:PAYLOAD, :] = lse_rows(lse)


SMEM = pl.BlockSpec(memory_space=pltpu.SMEM)
VMEM = pl.BlockSpec(memory_space=pltpu.VMEM)
HBM = pl.BlockSpec(memory_space=pltpu.HBM)


def state_shapes(count):
    return [(count, 1, ROWS), (count, 1, ROWS), (count, HD, ROWS)]


def buffers(nq, ns):
    return [
        pltpu.SMEM((nq * 4 * PER_SOURCE + 8,), jnp.int32),
        pltpu.SMEM((32, HD), jnp.int32),
        pltpu.VMEM((32, HD), jnp.int32),
        pltpu.VMEM((nq, ROWS, HD), BF16),
        pltpu.VMEM((nq, 16, HD), BF16),
        pltpu.VMEM((ns, SOURCE, HD), BF16),
    ]


def semaphores(nq, ns):
    return [
        pltpu.SemaphoreType.DMA((nq * (QPG + 1),)),
        pltpu.SemaphoreType.DMA((ns,)),
        pltpu.SemaphoreType.DMA,
    ]


def first_part(length, packed, sources, suffix_k, suffix_v):
    return pl.pallas_call(
        first_kernel,
        out_shape=[jax.ShapeDtypeStruct(s, F32) for s in state_shapes(NEAR + 1)],
        in_specs=[SMEM] + [HBM] * (NEAR + 2) + [VMEM] * 2,
        out_specs=[VMEM] * 3,
        scratch_shapes=buffers(NEAR, 2) + semaphores(NEAR, 2),
        compiler_params=pltpu.CompilerParams(vmem_limit_bytes=24 << 20),
        cost_estimate=pl.CostEstimate(
            flops=2_000_000_000, bytes_accessed=4 << 20, transcendentals=1_000_000
        ),
        name="first_part",
    )(length, *packed, *sources, suffix_k, suffix_v)


def second_part(packed, sources, known):
    nq = len(OFFSETS)
    return pl.pallas_call(
        second_kernel,
        out_shape=[
            jax.ShapeDtypeStruct((HD, ROWS), F32),
            jax.ShapeDtypeStruct((8, ROWS), F32),
        ]
        + [jax.ShapeDtypeStruct((PAYLOAD, ROWS), BF16)] * (nq - 1),
        in_specs=[HBM] * (nq + 7),
        out_specs=[VMEM] * (nq + 1),
        scratch_shapes=buffers(nq, 4)
        + [pltpu.VMEM(s, F32) for s in state_shapes(nq + 1)]
        + semaphores(nq, 4)
        + [pltpu.SemaphoreType.DMA((3,))],
        compiler_params=pltpu.CompilerParams(vmem_limit_bytes=24 << 20),
        cost_estimate=pl.CostEstimate(
            flops=4_000_000_000, bytes_accessed=6 << 20, transcendentals=3_000_000
        ),
        name="second_part",
    )(*packed, *sources, *known)


def join_kernel(place, ahead, back, from_ahead, from_back, from_far, ahead_out, back_out):
    odd = lax.bitwise_and(place[0], 1)
    for own, other, out, far_here in (
        (ahead, from_back, ahead_out, odd == 0),
        (back, from_ahead, back_out, odd == 1),
    ):
        parts = (own, other, from_far)
        lses = [lse_of(part[BLK:PAYLOAD, :]) for part in parts]
        lses[2] = jnp.where(far_here, lses[2], EMPTY)
        top = jnp.maximum(jnp.maximum(lses[0], lses[1]), lses[2])
        shares = [jnp.exp2(lse - top) for lse in lses]
        total = shares[0] + shares[1] + shares[2]
        inverse = 1.0 / total
        summed = parts[0][0:BLK, :].astype(F32) * (shares[0] * inverse)
        for part, share in zip(parts[1:], shares[1:]):
            summed = summed + part[0:BLK, :].astype(F32) * (share * inverse)
        out[0:BLK, :] = summed.astype(BF16)
        out[BLK:PAYLOAD, :] = lse_rows(jnp.maximum(top + jnp.log2(total), EMPTY))


def join(place, *parts):
    return pl.pallas_call(
        join_kernel,
        out_shape=[jax.ShapeDtypeStruct((PAYLOAD, ROWS), BF16)] * 2,
        in_specs=[SMEM] + [VMEM] * 5,
        out_specs=[VMEM] * 2,
        compiler_params=pltpu.CompilerParams(vmem_limit_bytes=16 << 20),
        cost_estimate=pl.CostEstimate(
            flops=2_000_000, bytes_accessed=1 << 20, transcendentals=4096
        ),
        name="join",
    )(place, *parts)


def projection_kernel(*refs):
    place, own_out, own_lse = refs[0:3]
    payloads = refs[3:7]
    weight = refs[7]
    shares = refs[8 : 8 + NX * NW]
    wbuf, sem = refs[8 + NX * NW :]
    width = wbuf.shape[2]
    here = place[0]
    x, w = lax.shift_right_logical(here, 1), lax.bitwise_and(here, 1)
    copies = []
    order = list(range(1, NX * NW)) + [0]
    for j, (dx, dw) in enumerate(RELATIVE):
        column = lax.bitwise_and(x + dx, NX - 1) * NW + lax.bitwise_and(w + dw, NW - 1)
        columns = pl.ds(pl.multiple_of(column * width, width), width)
        copies.append(pltpu.make_async_copy(weight.at[:, columns], wbuf.at[j], sem.at[j]))
    for j in order:
        copies[j].start()
    lses = [own_lse[0:1, :]] + [lse_of(payload[BLK:PAYLOAD, :]) for payload in payloads]
    top = lses[0]
    for lse in lses[1:]:
        top = jnp.maximum(top, lse)
    parts_of = [jnp.exp2(lse - top) for lse in lses]
    total = parts_of[0]
    for part in parts_of[1:]:
        total = total + part
    inverse = 1.0 / total
    mixed = own_out[...] * (parts_of[0] * inverse)
    for payload, part in zip(payloads, parts_of[1:]):
        mixed = mixed + payload[0:BLK, :].astype(F32) * (part * inverse)
    attended = jnp.concatenate(
        [mixed[:, h * BLK : (h + 1) * BLK].T for h in range(QPG)], axis=1
    ).astype(BF16)
    for j in order:
        copies[j].wait()
        shares[j][...] = jnp.dot(attended, wbuf[j], preferred_element_type=F32).astype(
            shares[j].dtype
        )


def projection(place, own_out, own_lse, payloads, weight):
    groups = NX * NW
    width = weight.shape[1] // groups
    return pl.pallas_call(
        projection_kernel,
        out_shape=[
            jax.ShapeDtypeStruct((BLK, width), F32 if j == 0 else BF16) for j in range(groups)
        ],
        in_specs=[SMEM] + [VMEM] * (2 + len(payloads)) + [HBM],
        out_specs=[VMEM] * groups,
        scratch_shapes=[
            pltpu.VMEM((groups, weight.shape[0], width), BF16),
            pltpu.SemaphoreType.DMA((groups,)),
        ],
        compiler_params=pltpu.CompilerParams(vmem_limit_bytes=54 << 20),
        cost_estimate=pl.CostEstimate(
            flops=1_100_000_000, bytes_accessed=10 << 20, transcendentals=4096
        ),
        name="projection",
    )(place, own_out, own_lse, *payloads, weight)


def shards(
    queries,
    cache_keys,
    cache_values,
    suffix_keys,
    suffix_values,
    out_weight,
    ancestor_mask,
    leaf_node,
    suffix_len,
):
    z = lax.bitwise_and(lax.shift_right_logical(lax.axis_index("cache"), 1), NZ - 1)
    z_place = z.astype(jnp.int32).reshape(1)
    head_place = lax.axis_index("heads").astype(jnp.int32).reshape(1)
    leaf_rows = jnp.broadcast_to(leaf_node.astype(BF16)[:, None], (16, ROWS))
    own = jnp.concatenate([queries, leaf_rows], axis=0)
    mask = jnp.pad(ancestor_mask.T.astype(BF16), ((0, 16 - PER_SOURCE), (0, HD - ancestor_mask.shape[0])))
    source = jnp.concatenate([cache_keys, cache_values, mask], axis=0)
    across = cache_step(source, 1, 0, 0)
    p1, m1 = cache_step(own, 0, -1, 0), cache_step(own, 0, 1, 0)
    p2, m2 = cache_step(own, 0, -2, 0), cache_step(own, 0, 2, 0)
    near = cache_step(source, 0, 0, 1)
    p3, m3 = cache_step(p2, 0, -1, 0), cache_step(m2, 0, 1, 0)
    p4 = z_ways(jnp.where(lax.bitwise_and(z, 1) == 0, m2, p2), 2, -2)
    known = first_part(
        suffix_len, [own, p1, m1, p2, m2], [source, near], suffix_keys, suffix_values
    )
    across, p3, m3, p4, *known = lax.optimization_barrier((across, p3, m3, p4, *known))
    far = cache_step(across, 0, 0, 1)
    own_out, own_lse, o_p1, o_m1, o_p2, o_m2, o_p3, o_m3, o_p4 = second_part(
        [own, p1, m1, p2, m2, p3, m3, p4], [source, near, across, far], known
    )
    from_far = z_ways(o_p4, 2, -2)
    from_back = cache_step(o_p3, 0, 1, 0)
    from_ahead = cache_step(o_m3, 0, -1, 0)
    r_p1, r_m1 = cache_step(o_p1, 0, 1, 0), cache_step(o_m1, 0, -1, 0)
    ahead, back = join(z_place, o_p2, o_m2, from_ahead, from_back, from_far)
    r_p2, r_m2 = cache_step(ahead, 0, 2, 0), cache_step(back, 0, -2, 0)
    shares = projection(head_place, own_out, own_lse, [r_p1, r_m1, r_p2, r_m2], out_weight)
    mixed = shares[0]
    for share, (dx, dw) in zip(shares[1:], RELATIVE[1:]):
        mixed = mixed + heads_step(share, dx, dw).astype(F32)
    return mixed.astype(BF16)


def solution(mesh):
    return jax.shard_map(
        shards,
        mesh=mesh,
        in_specs=(
            P("cache", "heads"),
            P("cache", "heads"),
            P("cache", "heads"),
            P("cache", "heads"),
            P("cache", "heads"),
            P("heads", None),
            P(None, "cache"),
            P("cache"),
            P("cache"),
        ),
        out_specs=P("cache", "heads"),
        check_vma=False,
    )
```

```python
import math

import jax
import jax.numpy as jnp
from jax import lax
from jax.experimental import pallas as pl
from jax.experimental.pallas import tpu as pltpu
from jax.sharding import PartitionSpec as P

BF16 = jnp.bfloat16
F32 = jnp.float32
NY, NZ, NC = 2, 8, 2
NX, NW = 4, 2
HD = 128
BLK = 128
QPG = 4
ROWS = QPG * BLK
EMPTY = -1e30
SCALE2 = math.log2(math.e) / math.sqrt(HD)
OFFSETS = (0, 1, -1, 2, -2, 3, -3, 4)
NEAR = 5
STEPS = (2, 1, 3, 0)
PAYLOAD = BLK + 16
PER_SOURCE = 12
KEYS_AT, VALUES_AT, MASK_AT = 0, PER_SOURCE * BLK, 2 * PER_SOURCE * BLK
SOURCE = MASK_AT + 16


def cache_step(x, dy, dz, dc):
    pairs = []
    for y in range(NY):
        for z in range(NZ):
            for c in range(NC):
                there = (((y + dy) % NY) * NZ + (z + dz) % NZ) * NC + (c + dc) % NC
                pairs.append(((y * NZ + z) * NC + c, there))
    return lax.ppermute(x, "cache", pairs)


def heads_step(x, dx, dw):
    pairs = []
    for a in range(NX):
        for w in range(NW):
            pairs.append((a * NW + w, ((a + dx) % NX) * NW + (w + dw) % NW))
    return lax.ppermute(x, "heads", pairs)


def z_ways(x, even, odd):
    pairs = []
    for y in range(NY):
        for z in range(NZ):
            for c in range(NC):
                there = (y * NZ + (z + (odd if z % 2 else even)) % NZ) * NC + c
                pairs.append(((y * NZ + z) * NC + c, there))
    return lax.ppermute(x, "cache", pairs)


def scores_of(keys, rows):
    return lax.dot_general(keys, rows, (((1,), (1,)), ((), ())), preferred_element_type=F32)


def weighted(values, weights):
    return lax.dot_general(
        values, weights.astype(BF16), (((0,), (0,)), ((), ())), preferred_element_type=F32
    )


def softmax_part(scores):
    peak = jnp.max(scores, axis=0, keepdims=True)
    weights = jnp.exp2((scores - peak) * SCALE2)
    return peak, jnp.sum(weights, axis=0, keepdims=True), weights


def fetch(packed, qbuf, qsem):
    copies = []
    for b, ref in enumerate(packed):
        for h in range(QPG):
            copies.append(
                pltpu.make_async_copy(
                    ref.at[pl.ds(0, BLK), pl.ds(h * HD, HD)],
                    qbuf.at[b, pl.ds(h * BLK, BLK), :],
                    qsem.at[b * QPG + h],
                )
            )
    for copy in copies:
        copy.start()
    return copies


def list_items(wanted, packed, sources, vis_v, vis_s, todo, dummy, vsem):
    blocks = sorted({b for b, _ in wanted})
    leaves = [packed[b][BLK:PAYLOAD, 0:HD].astype(F32)[0:1, :] for b in blocks]
    leaf = jnp.concatenate(leaves, axis=0)
    node_at = lax.broadcasted_iota(jnp.int32, leaf.shape, 1).astype(F32)
    chosen = jnp.where(node_at == leaf, 1.0, 0.0).astype(BF16)
    for s in sorted({s for _, s in wanted}):
        seen = scores_of(chosen, sources[s][MASK_AT:SOURCE, :])
        vis_v[8 * s : 8 * s + len(blocks), 0:16] = seen.astype(jnp.int32)
    copy = pltpu.make_async_copy(vis_v, vis_s, vsem)
    copy.start()
    copy.wait()
    count = jnp.int32(0)
    for b, s in wanted:
        for c in range(PER_SOURCE):
            todo[count] = b * 64 + s * 16 + c
            count = count + vis_s[8 * s + b, c]
    for i in range(6):
        todo[count + i] = dummy * 64
    return count


def work(count, todo, nq, qbuf, sources, state, ahead):
    def place(item):
        b = lax.shift_right_logical(item, 6)
        s = lax.bitwise_and(lax.shift_right_logical(item, 4), 3)
        return b, s, pl.multiple_of(lax.bitwise_and(item, 15) * BLK, BLK)

    def rows_of(s, row):
        rows = sources[0][pl.ds(row, BLK), :]
        for i in range(1, len(sources)):
            rows = jnp.where(s == i, sources[i][pl.ds(row, BLK), :], rows)
        return rows

    def scored(item):
        b, s, row = place(item)
        return scores_of(rows_of(s, row), qbuf[jnp.minimum(b, nq - 1)])

    def taken(item, scores):
        b, s, row = place(item)
        peak, total, weights = softmax_part(scores)
        return b, peak, total, weighted(rows_of(s, VALUES_AT + row), weights)

    def score_two(slot, at):
        ahead[slot, 0] = scored(todo[at])
        ahead[slot, 1] = scored(todo[at + 1])

    def take_two(slot, at):
        first = taken(todo[at], ahead[slot, 0])
        second = taken(todo[at + 1], ahead[slot, 1])
        merge(state, *first)
        merge(state, *second)

    def four(i, carry):
        score_two(1, 4 * i + 2)
        take_two(0, 4 * i)
        score_two(0, 4 * i + 4)
        take_two(1, 4 * i + 2)
        return carry

    score_two(0, 0)
    lax.fori_loop(0, lax.shift_right_logical(count + 3, 2), four, 0)


def merge(state, b, peak, total, summed):
    peaks, totals, sums = state
    before = peaks[b]
    after = jnp.maximum(before, peak)
    keep = jnp.exp2((before - after) * SCALE2)
    take = jnp.exp2((peak - after) * SCALE2)
    peaks[b] = after
    totals[b] = totals[b] * keep + total * take
    sums[b] = sums[b] * keep + summed * take


def column_copies(weight, out, sem, other_w):
    x = lax.shift_right_logical(lax.axis_index("heads"), 1)
    w = lax.bitwise_xor(lax.bitwise_and(lax.axis_index("heads"), 1), other_w)
    width = out.shape[2]
    copies = []
    for j, dx in enumerate(STEPS):
        column = lax.bitwise_and(x + dx, NX - 1) * NW + w
        columns = pl.ds(pl.multiple_of(column * width, width), width)
        copies.append(pltpu.make_async_copy(weight.at[:, columns], out.at[j], sem.at[j]))
    for copy in copies:
        copy.start()
    return copies


def early_kernel(length, own, suffix_k, suffix_v, weight, peak, total, summed, far_w, sem):
    copies = column_copies(weight, far_w, sem, 1)
    rows = jnp.concatenate([own[0:BLK, h * HD : (h + 1) * HD] for h in range(QPG)], axis=0)
    key_at = lax.broadcasted_iota(jnp.int32, (BLK, ROWS), 0)
    row_at = lax.bitwise_and(lax.broadcasted_iota(jnp.int32, (BLK, ROWS), 1), BLK - 1)
    scores = scores_of(suffix_k[...], rows)
    scores = jnp.where((key_at <= row_at) & (key_at < length[0]), scores, EMPTY)
    peak[...], total[...], weights = softmax_part(scores)
    summed[...] = weighted(suffix_v[...], weights)
    for copy in copies:
        copy.wait()


def laid_out(weight):
    return jax.ShapeDtypeStruct((NX, weight.shape[0], weight.shape[1] // (NX * NW)), BF16)


def early(length, own, suffix_k, suffix_v, weight):
    return pl.pallas_call(
        early_kernel,
        out_shape=[
            jax.ShapeDtypeStruct((1, ROWS), F32),
            jax.ShapeDtypeStruct((1, ROWS), F32),
            jax.ShapeDtypeStruct((HD, ROWS), F32),
            laid_out(weight),
        ],
        in_specs=[SMEM] + [VMEM] * 3 + [HBM],
        out_specs=[VMEM] * 4,
        scratch_shapes=[pltpu.SemaphoreType.DMA((NX,))],
        compiler_params=pltpu.CompilerParams(vmem_limit_bytes=46 << 20),
        cost_estimate=pl.CostEstimate(
            flops=40_000_000, bytes_accessed=9 << 20, transcendentals=70_000
        ),
        name="early",
    )(length, own, suffix_k, suffix_v, weight)


def late_kernel(weight, home_w, sem):
    for copy in column_copies(weight, home_w, sem, 0):
        copy.wait()


def late(weight):
    return pl.pallas_call(
        late_kernel,
        out_shape=laid_out(weight),
        in_specs=[HBM],
        out_specs=VMEM,
        scratch_shapes=[pltpu.SemaphoreType.DMA((NX,))],
        compiler_params=pltpu.CompilerParams(vmem_limit_bytes=46 << 20),
        cost_estimate=pl.CostEstimate(flops=0, bytes_accessed=8 << 20, transcendentals=0),
        name="late",
    )(weight)


def first_kernel(*refs):
    packed, sources = refs[0:NEAR], refs[NEAR : NEAR + 2]
    suffix = refs[NEAR + 2 : NEAR + 5]
    state = refs[NEAR + 5 : NEAR + 8]
    todo, vis_s, vis_v, qbuf, ahead, qsem, vsem = refs[NEAR + 8 :]
    copies = fetch(packed, qbuf, qsem)
    wanted = [(b, s) for b in range(NEAR) for s in range(2)]
    count = list_items(wanted, packed, sources, vis_v, vis_s, todo, NEAR, vsem)
    peaks, totals, sums = state
    peaks[0], totals[0], sums[0] = suffix[0][...], suffix[1][...], suffix[2][...]
    clear(state, range(1, NEAR + 1))
    for copy in copies:
        copy.wait()
    work(count, todo, NEAR, qbuf, sources, state, ahead)


def clear(state, blocks):
    peaks, totals, sums = state
    for b in blocks:
        peaks[b] = jnp.full((1, ROWS), EMPTY, F32)
        totals[b] = jnp.zeros((1, ROWS), F32)
        sums[b] = jnp.zeros((HD, ROWS), F32)


def lse_rows(lse):
    high = lse.astype(BF16).astype(F32)
    middle = (lse - high).astype(BF16).astype(F32)
    low = lse - high - middle
    at = lax.broadcasted_iota(jnp.int32, (16, ROWS), 0)
    return jnp.where(at == 0, high, jnp.where(at == 1, middle, low)).astype(BF16)


def lse_of(rows):
    pieces = rows.astype(F32)
    return pieces[0:1] + pieces[1:2] + pieces[2:3]


def second_kernel(*refs):
    nq = len(OFFSETS)
    packed, sources, known = refs[0:nq], refs[nq : nq + 4], refs[nq + 4 : nq + 7]
    own_out, own_lse, p_out, m_out, far_out, ahead_out, back_out = refs[nq + 7 : nq + 14]
    todo, vis_s, vis_v, qbuf, ahead, peaks, totals, sums, qsem, vsem = refs[nq + 14 :]
    state = (peaks, totals, sums)
    copies = fetch(packed, qbuf, qsem)
    wanted = [(b, s) for b in range(NEAR, nq) for s in range(4)]
    wanted += [(b, s) for b in range(NEAR) for s in (2, 3)]
    count = list_items(wanted, packed, sources, vis_v, vis_s, todo, nq, vsem)
    clear(state, range(nq + 1))
    for copy in copies:
        copy.wait()
    work(count, todo, nq, qbuf, sources, state, ahead)
    places = {1: (p_out, 0), 5: (p_out, PAYLOAD), 2: (m_out, 0), 6: (m_out, PAYLOAD)}
    places |= {7: (far_out, 0), 3: (ahead_out, 0), 4: (back_out, 0)}
    for b in (5, 6, 7, 1, 2, 3, 4, 0):
        if b < NEAR:
            merge(state, b, known[0][b], known[1][b], known[2][b])
        total = totals[b]
        seen = total > 0.0
        safe = jnp.where(seen, total, 1.0)
        lse = jnp.where(seen, peaks[b] * SCALE2 + jnp.log2(safe), EMPTY)
        out = sums[b] * (1.0 / safe)
        if b == 0:
            own_out[...] = out
            own_lse[...] = jnp.broadcast_to(lse, own_lse.shape)
        else:
            ref, at = places[b]
            ref[at : at + BLK, :] = out.astype(BF16)
            ref[at + BLK : at + PAYLOAD, :] = lse_rows(lse)


SMEM = pl.BlockSpec(memory_space=pltpu.SMEM)
VMEM = pl.BlockSpec(memory_space=pltpu.VMEM)
HBM = pl.BlockSpec(memory_space=pltpu.HBM)


def state_shapes(count):
    return [(count, 1, ROWS), (count, 1, ROWS), (count, HD, ROWS)]


def buffers(nq):
    return [
        pltpu.SMEM((nq * 4 * PER_SOURCE + 8,), jnp.int32),
        pltpu.SMEM((32, HD), jnp.int32),
        pltpu.VMEM((32, HD), jnp.int32),
        pltpu.VMEM((nq, ROWS, HD), BF16),
        pltpu.VMEM((2, 2, BLK, ROWS), F32),
    ]


def semaphores(nq):
    return [pltpu.SemaphoreType.DMA((nq * QPG,)), pltpu.SemaphoreType.DMA]


def first_part(packed, sources, suffix):
    return pl.pallas_call(
        first_kernel,
        out_shape=[jax.ShapeDtypeStruct(s, F32) for s in state_shapes(NEAR + 1)],
        in_specs=[VMEM] * (NEAR + 5),
        out_specs=[VMEM] * 3,
        scratch_shapes=buffers(NEAR) + semaphores(NEAR),
        compiler_params=pltpu.CompilerParams(vmem_limit_bytes=12 << 20),
        cost_estimate=pl.CostEstimate(
            flops=2_000_000_000, bytes_accessed=4 << 20, transcendentals=1_000_000
        ),
        name="first_part",
    )(*packed, *sources, *suffix)


def second_part(packed, sources, known):
    nq = len(OFFSETS)
    payload = jax.ShapeDtypeStruct((PAYLOAD, ROWS), BF16)
    double = jax.ShapeDtypeStruct((2 * PAYLOAD, ROWS), BF16)
    return pl.pallas_call(
        second_kernel,
        out_shape=[
            jax.ShapeDtypeStruct((HD, ROWS), F32),
            jax.ShapeDtypeStruct((8, ROWS), F32),
            double,
            double,
            payload,
            payload,
            payload,
        ],
        in_specs=[VMEM] * (nq + 7),
        out_specs=[VMEM] * 7,
        scratch_shapes=buffers(nq)
        + [pltpu.VMEM(s, F32) for s in state_shapes(nq + 1)]
        + semaphores(nq),
        compiler_params=pltpu.CompilerParams(vmem_limit_bytes=16 << 20),
        cost_estimate=pl.CostEstimate(
            flops=4_000_000_000, bytes_accessed=6 << 20, transcendentals=3_000_000
        ),
        name="second_part",
    )(*packed, *sources, *known)


def join_kernel(ahead, back, from_ahead, from_back, from_far, ahead_out, back_out):
    odd = lax.bitwise_and(lax.shift_right_logical(lax.axis_index("cache"), 1), 1)
    from_ahead, from_back = from_ahead.at[PAYLOAD:], from_back.at[PAYLOAD:]
    for own, other, out, far_here in (
        (ahead, from_back, ahead_out, odd == 0),
        (back, from_ahead, back_out, odd == 1),
    ):
        parts = (own, other, from_far)
        lses = [lse_of(part[BLK:PAYLOAD, :]) for part in parts]
        lses[2] = jnp.where(far_here, lses[2], EMPTY)
        top = jnp.maximum(jnp.maximum(lses[0], lses[1]), lses[2])
        shares = [jnp.exp2(lse - top) for lse in lses]
        total = shares[0] + shares[1] + shares[2]
        inverse = 1.0 / total
        summed = parts[0][0:BLK, :].astype(F32) * (shares[0] * inverse)
        for part, share in zip(parts[1:], shares[1:]):
            summed = summed + part[0:BLK, :].astype(F32) * (share * inverse)
        out[0:BLK, :] = summed.astype(BF16)
        out[BLK:PAYLOAD, :] = lse_rows(jnp.maximum(top + jnp.log2(total), EMPTY))


def join(*parts):
    return pl.pallas_call(
        join_kernel,
        out_shape=[jax.ShapeDtypeStruct((PAYLOAD, ROWS), BF16)] * 2,
        in_specs=[VMEM] * 5,
        out_specs=[VMEM] * 2,
        compiler_params=pltpu.CompilerParams(vmem_limit_bytes=6 << 20),
        cost_estimate=pl.CostEstimate(
            flops=2_000_000, bytes_accessed=1 << 20, transcendentals=4096
        ),
        name="join",
    )(*parts)


def merged_rows(own_out, own_lse, payloads):
    lses = [own_lse[0:1, :]] + [lse_of(payload[BLK:PAYLOAD, :]) for payload in payloads]
    top = lses[0]
    for lse in lses[1:]:
        top = jnp.maximum(top, lse)
    parts_of = [jnp.exp2(lse - top) for lse in lses]
    total = parts_of[0]
    for part in parts_of[1:]:
        total = total + part
    inverse = 1.0 / total
    mixed = own_out[...] * (parts_of[0] * inverse)
    for payload, part in zip(payloads, parts_of[1:]):
        mixed = mixed + payload[0:BLK, :].astype(F32) * (part * inverse)
    return mixed


def project(rows, weight, outs):
    tile = 256
    for j, out in enumerate(outs):
        for t in range(weight.shape[2] // tile):
            columns = slice(t * tile, (t + 1) * tile)
            out[:, columns] = jnp.dot(
                rows, weight[j, :, columns], preferred_element_type=F32
            ).astype(out.dtype)


def away_kernel(own_out, own_lse, p1, m1, p2, m2, weight, rows_out, *outs):
    mixed = merged_rows(own_out, own_lse, (p1, m1, p2, m2))
    for h in range(QPG):
        columns = slice(h * BLK, (h + 1) * BLK)
        rows_out[:, columns] = mixed[:, columns].T.astype(BF16)
    project(rows_out[...], weight, outs)


def home_kernel(rows, weight, *outs):
    project(rows[...], weight, outs)


def projected(kernel, name, operands, weight, more):
    return pl.pallas_call(
        kernel,
        out_shape=more
        + [jax.ShapeDtypeStruct((BLK, weight.shape[2]), F32 if dx == 0 else BF16) for dx in STEPS],
        in_specs=[VMEM] * (len(operands) + 1),
        out_specs=[VMEM] * (len(more) + NX),
        compiler_params=pltpu.CompilerParams(vmem_limit_bytes=12 << 20),
        cost_estimate=pl.CostEstimate(
            flops=550_000_000, bytes_accessed=5 << 20, transcendentals=4096
        ),
        name=name,
    )(*operands, weight)


def add_kernel(first, *refs):
    others, out = refs[:-1], refs[-1]
    total = first[...]
    for other in others:
        total = total + other[...].astype(F32)
    out[...] = total.astype(out.dtype)


def sum_of(name, first, others):
    return pl.pallas_call(
        add_kernel,
        out_shape=jax.ShapeDtypeStruct(first.shape, BF16),
        in_specs=[VMEM] * (1 + len(others)),
        out_specs=VMEM,
        compiler_params=pltpu.CompilerParams(vmem_limit_bytes=6 << 20),
        cost_estimate=pl.CostEstimate(
            flops=1_000_000, bytes_accessed=2 << 20, transcendentals=0
        ),
        name=name,
    )(first, *others)


def shards(
    queries,
    cache_keys,
    cache_values,
    suffix_keys,
    suffix_values,
    out_weight,
    ancestor_mask,
    leaf_node,
    suffix_len,
):
    z = lax.bitwise_and(lax.shift_right_logical(lax.axis_index("cache"), 1), NZ - 1)
    leaf_rows = jnp.broadcast_to(leaf_node.astype(BF16)[:, None], (16, ROWS))
    own = jnp.concatenate([queries, leaf_rows], axis=0)
    count, nodes = ancestor_mask.shape[1], ancestor_mask.shape[0]
    mask = jnp.pad(ancestor_mask.T.astype(BF16), ((0, 16 - count), (0, HD - nodes)))
    source = jnp.concatenate([cache_keys, cache_values, mask], axis=0)
    across = cache_step(source, 1, 0, 0)
    p2, m2 = cache_step(own, 0, -2, 0), cache_step(own, 0, 2, 0)
    near = cache_step(source, 0, 0, 1)
    near, own = lax.optimization_barrier((near, own))
    p1, m1 = cache_step(own, 0, -1, 0), cache_step(own, 0, 1, 0)
    *suffix, far_w = early(suffix_len, own, suffix_keys, suffix_values, out_weight)
    p2, m2, *suffix = lax.optimization_barrier((p2, m2, *suffix))
    p3, m3 = cache_step(p2, 0, -1, 0), cache_step(m2, 0, 1, 0)
    p4 = z_ways(jnp.where(lax.bitwise_and(z, 1) == 0, m2, p2), 2, -2)
    known = first_part([own, p1, m1, p2, m2], [source, near], suffix)
    across, p3, m3, p4, *known = lax.optimization_barrier((across, p3, m3, p4, *known))
    far = cache_step(across, 0, 0, 1)
    own_out, own_lse, o_p, o_m, o_far, o_p2, o_m2 = second_part(
        [own, p1, m1, p2, m2, p3, m3, p4], [source, near, across, far], known
    )
    from_far = z_ways(o_far, 2, -2)
    later_weight, own_lse = lax.optimization_barrier((out_weight, own_lse))
    home_w = late(later_weight)
    from_back, from_ahead = cache_step(o_p, 0, 1, 0), cache_step(o_m, 0, -1, 0)
    from_far, home_w = lax.optimization_barrier((from_far, home_w))
    ahead, back = join(o_p2, o_m2, from_ahead, from_back, from_far)
    r_p2, r_m2 = cache_step(ahead, 0, 2, 0), cache_step(back, 0, -2, 0)
    merged, *shares = projected(
        away_kernel,
        "away",
        [own_out, own_lse, from_back, from_ahead, r_p2, r_m2],
        far_w,
        [jax.ShapeDtypeStruct((BLK, ROWS), BF16)],
    )
    arrived = [heads_step(share, dx, 0) for share, dx in zip(shares[:-1], STEPS)]
    kept = projected(home_kernel, "home", [merged], home_w, [])
    passed = heads_step(sum_of("pass_on", shares[-1], arrived), 0, 1)
    arrived = [heads_step(share, dx, 0) for share, dx in zip(kept[:-1], STEPS)]
    return sum_of("finish", kept[-1], [*arrived, passed])


def solution(mesh):
    return jax.shard_map(
        shards,
        mesh=mesh,
        in_specs=(
            P("cache", "heads"),
            P("cache", "heads"),
            P("cache", "heads"),
            P("cache", "heads"),
            P("cache", "heads"),
            P("heads", None),
            P(None, "cache"),
            P("cache"),
            P("cache"),
        ),
        out_specs=P("cache", "heads"),
        check_vma=False,
    )
```

```python
import functools
import math

import jax
import jax.numpy as jnp
from jax import lax
from jax.experimental import pallas as pl
from jax.experimental.pallas import tpu as pltpu
from jax.sharding import PartitionSpec as P

BF16 = jnp.bfloat16
F32 = jnp.float32
NY, NZ, NC = 2, 8, 2
NX, NW = 4, 2
HD = 128
BLK = 128
QPG = 4
ROWS = QPG * BLK
EMPTY = -1e30
SCALE2 = math.log2(math.e) / math.sqrt(HD)
OFFSETS = (0, 1, -1, 2, -2, 3, -3, 4)
NEAR = 5
STEPS = (2, 1, 3, 0)
PAYLOAD = BLK + 16
PER_SOURCE = 12
KEYS_AT, VALUES_AT, MASK_AT = 0, PER_SOURCE * BLK, 2 * PER_SOURCE * BLK
SOURCE = MASK_AT + 16


def cache_step(x, dy, dz, dc):
    pairs = []
    for y in range(NY):
        for z in range(NZ):
            for c in range(NC):
                there = (((y + dy) % NY) * NZ + (z + dz) % NZ) * NC + (c + dc) % NC
                pairs.append(((y * NZ + z) * NC + c, there))
    return lax.ppermute(x, "cache", pairs)


def heads_step(x, dx, dw):
    pairs = []
    for a in range(NX):
        for w in range(NW):
            pairs.append((a * NW + w, ((a + dx) % NX) * NW + (w + dw) % NW))
    return lax.ppermute(x, "heads", pairs)


def z_ways(x, even, odd):
    pairs = []
    for y in range(NY):
        for z in range(NZ):
            for c in range(NC):
                there = (y * NZ + (z + (odd if z % 2 else even)) % NZ) * NC + c
                pairs.append(((y * NZ + z) * NC + c, there))
    return lax.ppermute(x, "cache", pairs)


def scores_of(keys, rows):
    return lax.dot_general(keys, rows, (((1,), (1,)), ((), ())), preferred_element_type=F32)


def weighted(values, weights):
    return lax.dot_general(
        values, weights.astype(BF16), (((0,), (0,)), ((), ())), preferred_element_type=F32
    )


def softmax_part(scores):
    peak = jnp.max(scores, axis=0, keepdims=True)
    weights = jnp.exp2((scores - peak) * SCALE2)
    return peak, jnp.sum(weights, axis=0, keepdims=True), weights


def fetch(packed, qbuf, qsem):
    copies = []
    for b, ref in enumerate(packed):
        for h in range(QPG):
            copies.append(
                pltpu.make_async_copy(
                    ref.at[pl.ds(0, BLK), pl.ds(h * HD, HD)],
                    qbuf.at[b, pl.ds(h * BLK, BLK), :],
                    qsem.at[b * QPG + h],
                )
            )
    for copy in copies:
        copy.start()
    return copies


def list_items(wanted, packed, sources, vis_v, vis_s, todo, dummy, vsem):
    blocks = sorted({b for b, _ in wanted})
    leaves = [packed[b][BLK:PAYLOAD, 0:HD].astype(F32)[0:1, :] for b in blocks]
    leaf = jnp.concatenate(leaves, axis=0)
    node_at = lax.broadcasted_iota(jnp.int32, leaf.shape, 1).astype(F32)
    chosen = jnp.where(node_at == leaf, 1.0, 0.0).astype(BF16)
    for s in sorted({s for _, s in wanted}):
        seen = scores_of(chosen, sources[s][MASK_AT:SOURCE, :])
        vis_v[8 * s : 8 * s + len(blocks), 0:16] = seen.astype(jnp.int32)
    copy = pltpu.make_async_copy(vis_v, vis_s, vsem)
    copy.start()
    copy.wait()
    count = jnp.int32(0)
    for b, s in wanted:
        for c in range(PER_SOURCE):
            todo[count] = b * 64 + s * 16 + c
            count = count + vis_s[8 * s + b, c]
    for i in range(6):
        todo[count + i] = dummy * 64
    return count


def work(count, todo, nq, qbuf, sources, state, ahead):
    def place(item):
        b = lax.shift_right_logical(item, 6)
        s = lax.bitwise_and(lax.shift_right_logical(item, 4), 3)
        return b, s, pl.multiple_of(lax.bitwise_and(item, 15) * BLK, BLK)

    def rows_of(s, row):
        rows = sources[0][pl.ds(row, BLK), :]
        for i in range(1, len(sources)):
            rows = jnp.where(s == i, sources[i][pl.ds(row, BLK), :], rows)
        return rows

    def scored(item):
        b, s, row = place(item)
        return scores_of(rows_of(s, row), qbuf[jnp.minimum(b, nq - 1)])

    def taken(item, scores):
        b, s, row = place(item)
        peak, total, weights = softmax_part(scores)
        return b, peak, total, weighted(rows_of(s, VALUES_AT + row), weights)

    def score_two(slot, at):
        ahead[slot, 0] = scored(todo[at])
        ahead[slot, 1] = scored(todo[at + 1])

    def take_two(slot, at):
        first = taken(todo[at], ahead[slot, 0])
        second = taken(todo[at + 1], ahead[slot, 1])
        merge(state, *first)
        merge(state, *second)

    def four(i, carry):
        score_two(1, 4 * i + 2)
        take_two(0, 4 * i)
        score_two(0, 4 * i + 4)
        take_two(1, 4 * i + 2)
        return carry

    score_two(0, 0)
    lax.fori_loop(0, lax.shift_right_logical(count + 3, 2), four, 0)


def merge(state, b, peak, total, summed):
    peaks, totals, sums = state
    before = peaks[b]
    after = jnp.maximum(before, peak)
    keep = jnp.exp2((before - after) * SCALE2)
    take = jnp.exp2((peak - after) * SCALE2)
    peaks[b] = after
    totals[b] = totals[b] * keep + total * take
    sums[b] = sums[b] * keep + summed * take


def column_copies(weight, out, sem, other_w, steps):
    x = lax.shift_right_logical(lax.axis_index("heads"), 1)
    w = lax.bitwise_xor(lax.bitwise_and(lax.axis_index("heads"), 1), other_w)
    width = out.shape[2]
    copies = []
    for j, dx in enumerate(steps):
        column = lax.bitwise_and(x + dx, NX - 1) * NW + w
        columns = pl.ds(pl.multiple_of(column * width, width), width)
        copies.append(pltpu.make_async_copy(weight.at[:, columns], out.at[j], sem.at[j]))
    for copy in copies:
        copy.start()
    return copies


def early_kernel(
    length, own, suffix_k, suffix_v, weight, peak, total, summed, far_w, home_w, sem, home_sem
):
    copies = column_copies(weight, far_w, sem, 1, STEPS)
    copies += column_copies(weight, home_w, home_sem, 0, STEPS[:-1])
    rows = jnp.concatenate([own[0:BLK, h * HD : (h + 1) * HD] for h in range(QPG)], axis=0)
    key_at = lax.broadcasted_iota(jnp.int32, (BLK, ROWS), 0)
    row_at = lax.bitwise_and(lax.broadcasted_iota(jnp.int32, (BLK, ROWS), 1), BLK - 1)
    scores = scores_of(suffix_k[...], rows)
    scores = jnp.where((key_at <= row_at) & (key_at < length[0]), scores, EMPTY)
    peak[...], total[...], weights = softmax_part(scores)
    summed[...] = weighted(suffix_v[...], weights)
    for copy in copies:
        copy.wait()


def laid_out(weight, steps):
    shape = (len(steps), weight.shape[0], weight.shape[1] // (NX * NW))
    return jax.ShapeDtypeStruct(shape, BF16)


def early(length, own, suffix_k, suffix_v, weight):
    return pl.pallas_call(
        early_kernel,
        out_shape=[
            jax.ShapeDtypeStruct((1, ROWS), F32),
            jax.ShapeDtypeStruct((1, ROWS), F32),
            jax.ShapeDtypeStruct((HD, ROWS), F32),
            laid_out(weight, STEPS),
            laid_out(weight, STEPS[:-1]),
        ],
        in_specs=[SMEM] + [VMEM] * 3 + [HBM],
        out_specs=[VMEM] * 5,
        scratch_shapes=[
            pltpu.SemaphoreType.DMA((len(STEPS),)),
            pltpu.SemaphoreType.DMA((len(STEPS) - 1,)),
        ],
        compiler_params=pltpu.CompilerParams(vmem_limit_bytes=46 << 20),
        cost_estimate=pl.CostEstimate(
            flops=40_000_000, bytes_accessed=9 << 20, transcendentals=70_000
        ),
        name="early",
    )(length, own, suffix_k, suffix_v, weight)


def late_kernel(steps, weight, home_w, sem):
    for copy in column_copies(weight, home_w, sem, 0, steps):
        copy.wait()


def late(name, weight, steps):
    return pl.pallas_call(
        functools.partial(late_kernel, steps),
        out_shape=laid_out(weight, steps),
        in_specs=[HBM],
        out_specs=VMEM,
        scratch_shapes=[pltpu.SemaphoreType.DMA((len(steps),))],
        compiler_params=pltpu.CompilerParams(vmem_limit_bytes=46 << 20),
        cost_estimate=pl.CostEstimate(flops=0, bytes_accessed=8 << 20, transcendentals=0),
        name=name,
    )(weight)


def first_kernel(*refs):
    packed, sources = refs[0:NEAR], refs[NEAR : NEAR + 2]
    suffix = refs[NEAR + 2 : NEAR + 5]
    state = refs[NEAR + 5 : NEAR + 8]
    todo, vis_s, vis_v, qbuf, ahead, qsem, vsem = refs[NEAR + 8 :]
    copies = fetch(packed, qbuf, qsem)
    wanted = [(b, s) for b in range(NEAR) for s in range(2)]
    count = list_items(wanted, packed, sources, vis_v, vis_s, todo, NEAR, vsem)
    peaks, totals, sums = state
    peaks[0], totals[0], sums[0] = suffix[0][...], suffix[1][...], suffix[2][...]
    clear(state, range(1, NEAR + 1))
    for copy in copies:
        copy.wait()
    work(count, todo, NEAR, qbuf, sources, state, ahead)


def clear(state, blocks):
    peaks, totals, sums = state
    for b in blocks:
        peaks[b] = jnp.full((1, ROWS), EMPTY, F32)
        totals[b] = jnp.zeros((1, ROWS), F32)
        sums[b] = jnp.zeros((HD, ROWS), F32)


def lse_rows(lse):
    high = lse.astype(BF16).astype(F32)
    middle = (lse - high).astype(BF16).astype(F32)
    low = lse - high - middle
    at = lax.broadcasted_iota(jnp.int32, (16, ROWS), 0)
    return jnp.where(at == 0, high, jnp.where(at == 1, middle, low)).astype(BF16)


def lse_of(rows):
    pieces = rows.astype(F32)
    return pieces[0:1] + pieces[1:2] + pieces[2:3]


def solve(wanted, packed, sources, scratch):
    todo, vis_s, vis_v, qbuf, ahead, peaks, totals, sums, qsem, vsem = scratch
    nq, state = len(packed), (peaks, totals, sums)
    copies = fetch(packed, qbuf, qsem)
    count = list_items(wanted, packed, sources, vis_v, vis_s, todo, nq, vsem)
    clear(state, range(nq + 1))
    for copy in copies:
        copy.wait()
    work(count, todo, nq, qbuf, sources, state, ahead)
    return state


def outcome(state, b):
    peaks, totals, sums = state
    total = totals[b]
    seen = total > 0.0
    safe = jnp.where(seen, total, 1.0)
    lse = jnp.where(seen, peaks[b] * SCALE2 + jnp.log2(safe), EMPTY)
    return sums[b] * (1.0 / safe), lse


def write_payload(state, b, ref):
    out, lse = outcome(state, b)
    ref[0:BLK, :] = out.astype(BF16)
    ref[BLK:PAYLOAD, :] = lse_rows(lse)


def far_kernel(*refs):
    packed, sources, state, scratch = refs[0:3], refs[3:6], refs[6:9], refs[9:]
    wanted = [(b, s) for b in range(3) for s in range(3)]
    solve(wanted, packed, sources, (*scratch[0:5], *state, *scratch[5:]))


def last_kernel(*refs):
    packed, sources, known, outs, scratch = refs[0:3], refs[3:4], refs[4:7], refs[7:10], refs[10:]
    state = solve([(b, 0) for b in range(3)], packed, sources, scratch)
    for b, ref in enumerate(outs):
        merge(state, b, known[0][b], known[1][b], known[2][b])
        write_payload(state, b, ref)


def near_kernel(*refs):
    packed, sources = refs[0:NEAR], refs[NEAR : NEAR + 2]
    known, outs = refs[NEAR + 2 : NEAR + 5], refs[NEAR + 5 : 2 * NEAR + 6]
    state = solve(
        [(b, s) for b in range(NEAR) for s in range(2)], packed, sources, refs[2 * NEAR + 6 :]
    )
    for b in range(NEAR):
        merge(state, b, known[0][b], known[1][b], known[2][b])
        if b == 0:
            out, lse = outcome(state, b)
            outs[0][...] = out
            outs[1][...] = jnp.broadcast_to(lse, outs[1].shape)
        else:
            write_payload(state, b, outs[b + 1])


SMEM = pl.BlockSpec(memory_space=pltpu.SMEM)
VMEM = pl.BlockSpec(memory_space=pltpu.VMEM)
HBM = pl.BlockSpec(memory_space=pltpu.HBM)


def state_shapes(count):
    return [(count, 1, ROWS), (count, 1, ROWS), (count, HD, ROWS)]


def buffers(nq):
    return [
        pltpu.SMEM((nq * 4 * PER_SOURCE + 8,), jnp.int32),
        pltpu.SMEM((32, HD), jnp.int32),
        pltpu.VMEM((32, HD), jnp.int32),
        pltpu.VMEM((nq, ROWS, HD), BF16),
        pltpu.VMEM((2, 2, BLK, ROWS), F32),
    ]


def semaphores(nq):
    return [pltpu.SemaphoreType.DMA((nq * QPG,)), pltpu.SemaphoreType.DMA]


def first_part(packed, sources, suffix):
    return pl.pallas_call(
        first_kernel,
        out_shape=[jax.ShapeDtypeStruct(s, F32) for s in state_shapes(NEAR + 1)],
        in_specs=[VMEM] * (NEAR + 5),
        out_specs=[VMEM] * 3,
        scratch_shapes=buffers(NEAR) + semaphores(NEAR),
        compiler_params=pltpu.CompilerParams(vmem_limit_bytes=12 << 20),
        cost_estimate=pl.CostEstimate(
            flops=2_000_000_000, bytes_accessed=4 << 20, transcendentals=1_000_000
        ),
        name="first_part",
    )(*packed, *sources, *suffix)


def solved(kernel, name, packed, sources, known, outs, flops, own_state):
    nq = len(packed)
    scratch = buffers(nq) + semaphores(nq)
    if own_state:
        scratch[5:5] = [pltpu.VMEM(s, F32) for s in state_shapes(nq + 1)]
    return pl.pallas_call(
        kernel,
        out_shape=outs,
        in_specs=[VMEM] * (nq + len(sources) + len(known)),
        out_specs=[VMEM] * len(outs),
        scratch_shapes=scratch,
        compiler_params=pltpu.CompilerParams(vmem_limit_bytes=14 << 20),
        cost_estimate=pl.CostEstimate(
            flops=flops, bytes_accessed=4 << 20, transcendentals=2_000_000
        ),
        name=name,
    )(*packed, *sources, *known)


def far_part(packed, sources):
    outs = [jax.ShapeDtypeStruct(s, F32) for s in state_shapes(len(packed) + 1)]
    return solved(far_kernel, "far_part", packed, sources, [], outs, 20_000_000_000, False)


def last_part(packed, sources, known):
    outs = [jax.ShapeDtypeStruct((PAYLOAD, ROWS), BF16)] * len(packed)
    return solved(last_kernel, "last_part", packed, sources, known, outs, 1_500_000_000, True)


def near_part(packed, sources, known):
    outs = [jax.ShapeDtypeStruct((HD, ROWS), F32), jax.ShapeDtypeStruct((8, ROWS), F32)]
    outs += [jax.ShapeDtypeStruct((PAYLOAD, ROWS), BF16)] * (len(packed) - 1)
    return solved(
        near_kernel, "near_part", packed, sources, known, outs, 2_500_000_000, True
    )


def join_kernel(ahead, back, from_ahead, from_back, from_far, ahead_out, back_out):
    odd = lax.bitwise_and(lax.shift_right_logical(lax.axis_index("cache"), 1), 1)
    for own, other, out, far_here in (
        (ahead, from_back, ahead_out, odd == 0),
        (back, from_ahead, back_out, odd == 1),
    ):
        parts = (own, other, from_far)
        lses = [lse_of(part[BLK:PAYLOAD, :]) for part in parts]
        lses[2] = jnp.where(far_here, lses[2], EMPTY)
        top = jnp.maximum(jnp.maximum(lses[0], lses[1]), lses[2])
        shares = [jnp.exp2(lse - top) for lse in lses]
        total = shares[0] + shares[1] + shares[2]
        inverse = 1.0 / total
        summed = parts[0][0:BLK, :].astype(F32) * (shares[0] * inverse)
        for part, share in zip(parts[1:], shares[1:]):
            summed = summed + part[0:BLK, :].astype(F32) * (share * inverse)
        out[0:BLK, :] = summed.astype(BF16)
        out[BLK:PAYLOAD, :] = lse_rows(jnp.maximum(top + jnp.log2(total), EMPTY))


def join(*parts):
    return pl.pallas_call(
        join_kernel,
        out_shape=[jax.ShapeDtypeStruct((PAYLOAD, ROWS), BF16)] * 2,
        in_specs=[VMEM] * 5,
        out_specs=[VMEM] * 2,
        compiler_params=pltpu.CompilerParams(vmem_limit_bytes=6 << 20),
        cost_estimate=pl.CostEstimate(
            flops=2_000_000, bytes_accessed=1 << 20, transcendentals=4096
        ),
        name="join",
    )(*parts)


def merged_rows(own_out, own_lse, payloads):
    lses = [own_lse[0:1, :]] + [lse_of(payload[BLK:PAYLOAD, :]) for payload in payloads]
    top = lses[0]
    for lse in lses[1:]:
        top = jnp.maximum(top, lse)
    parts_of = [jnp.exp2(lse - top) for lse in lses]
    total = parts_of[0]
    for part in parts_of[1:]:
        total = total + part
    inverse = 1.0 / total
    mixed = own_out[...] * (parts_of[0] * inverse)
    for payload, part in zip(payloads, parts_of[1:]):
        mixed = mixed + payload[0:BLK, :].astype(F32) * (part * inverse)
    return mixed


def project(rows, weights, outs):
    tile = 256
    for weight, out in zip(weights, outs):
        for t in range(weight.shape[1] // tile):
            columns = slice(t * tile, (t + 1) * tile)
            out[:, columns] = jnp.dot(
                rows, weight[:, columns], preferred_element_type=F32
            ).astype(out.dtype)


def away_kernel(own_out, own_lse, p1, m1, p2, m2, weight, rows_out, *outs):
    mixed = merged_rows(own_out, own_lse, (p1, m1, p2, m2))
    for h in range(QPG):
        columns = slice(h * BLK, (h + 1) * BLK)
        rows_out[:, columns] = mixed[:, columns].T.astype(BF16)
    project(rows_out[...], [weight.at[j] for j in range(len(outs))], outs)


def home_kernel(rows, weight, own_weight, *outs):
    weights = [weight.at[j] for j in range(len(outs) - 1)] + [own_weight.at[0]]
    project(rows[...], weights, outs)


def projected(kernel, name, operands, more):
    width = operands[-1].shape[2]
    return pl.pallas_call(
        kernel,
        out_shape=more
        + [jax.ShapeDtypeStruct((BLK, width), F32 if dx == 0 else BF16) for dx in STEPS],
        in_specs=[VMEM] * len(operands),
        out_specs=[VMEM] * (len(more) + len(STEPS)),
        compiler_params=pltpu.CompilerParams(vmem_limit_bytes=12 << 20),
        cost_estimate=pl.CostEstimate(
            flops=550_000_000, bytes_accessed=5 << 20, transcendentals=4096
        ),
        name=name,
    )(*operands)


def add_kernel(first, *refs):
    others, out = refs[:-1], refs[-1]
    total = first[...]
    for other in others:
        total = total + other[...].astype(F32)
    out[...] = total.astype(out.dtype)


def sum_of(name, first, others):
    return pl.pallas_call(
        add_kernel,
        out_shape=jax.ShapeDtypeStruct(first.shape, BF16),
        in_specs=[VMEM] * (1 + len(others)),
        out_specs=VMEM,
        compiler_params=pltpu.CompilerParams(vmem_limit_bytes=6 << 20),
        cost_estimate=pl.CostEstimate(
            flops=1_000_000, bytes_accessed=2 << 20, transcendentals=0
        ),
        name=name,
    )(first, *others)


def shards(
    queries,
    cache_keys,
    cache_values,
    suffix_keys,
    suffix_values,
    out_weight,
    ancestor_mask,
    leaf_node,
    suffix_len,
):
    z = lax.bitwise_and(lax.shift_right_logical(lax.axis_index("cache"), 1), NZ - 1)
    leaf_rows = jnp.broadcast_to(leaf_node.astype(BF16)[:, None], (16, ROWS))
    own = jnp.concatenate([queries, leaf_rows], axis=0)
    count, nodes = ancestor_mask.shape[1], ancestor_mask.shape[0]
    mask = jnp.pad(ancestor_mask.T.astype(BF16), ((0, 16 - count), (0, HD - nodes)))
    source = jnp.concatenate([cache_keys, cache_values, mask], axis=0)
    across = cache_step(source, 1, 0, 0)
    p2, m2 = cache_step(own, 0, -2, 0), cache_step(own, 0, 2, 0)
    near = cache_step(source, 0, 0, 1)
    near, own = lax.optimization_barrier((near, own))
    p1, m1 = cache_step(own, 0, -1, 0), cache_step(own, 0, 1, 0)
    *suffix, far_w, home_w = early(suffix_len, own, suffix_keys, suffix_values, out_weight)
    p2, m2, *suffix = lax.optimization_barrier((p2, m2, *suffix))
    p3, m3 = cache_step(p2, 0, -1, 0), cache_step(m2, 0, 1, 0)
    p4 = z_ways(jnp.where(lax.bitwise_and(z, 1) == 0, m2, p2), 2, -2)
    known = first_part([own, p1, m1, p2, m2], [source, near], suffix)
    across, *known = lax.optimization_barrier((across, *known))
    far = cache_step(across, 0, 0, 1)
    far_known = far_part([p3, m3, p4], [source, near, across])
    o_p3, o_m3, o_p4 = last_part([p3, m3, p4], [far], far_known)
    from_far = z_ways(o_p4, 2, -2)
    from_back, from_ahead = cache_step(o_p3, 0, 1, 0), cache_step(o_m3, 0, -1, 0)
    o_p4, *known = lax.optimization_barrier((o_p4, *known))
    own_out, own_lse, o_p1, o_m1, o_p2, o_m2 = near_part(
        [own, p1, m1, p2, m2], [across, far], known
    )
    r_p1, r_m1 = cache_step(o_p1, 0, 1, 0), cache_step(o_m1, 0, -1, 0)
    near_weight, own_lse = lax.optimization_barrier((out_weight, own_lse))
    own_w = late("late_own", near_weight, STEPS[-1:])
    from_far, own_w = lax.optimization_barrier((from_far, own_w))
    ahead, back = join(o_p2, o_m2, from_ahead, from_back, from_far)
    r_p2, r_m2 = cache_step(ahead, 0, 2, 0), cache_step(back, 0, -2, 0)
    merged, *shares = projected(
        away_kernel,
        "away",
        [own_out, own_lse, r_p1, r_m1, r_p2, r_m2, far_w],
        [jax.ShapeDtypeStruct((BLK, ROWS), BF16)],
    )
    arrived = [heads_step(share, dx, 0) for share, dx in zip(shares[:-1], STEPS)]
    kept = projected(home_kernel, "home", [merged, home_w, own_w], [])
    passed = heads_step(sum_of("pass_on", shares[-1], arrived), 0, 1)
    arrived = [heads_step(share, dx, 0) for share, dx in zip(kept[:-1], STEPS)]
    return sum_of("finish", kept[-1], [*arrived, passed])


def solution(mesh):
    return jax.shard_map(
        shards,
        mesh=mesh,
        in_specs=(
            P("cache", "heads"),
            P("cache", "heads"),
            P("cache", "heads"),
            P("cache", "heads"),
            P("cache", "heads"),
            P("heads", None),
            P(None, "cache"),
            P("cache"),
            P("cache"),
        ),
        out_specs=P("cache", "heads"),
        check_vma=False,
    )
```

```python
import functools
import math

import jax
import jax.numpy as jnp
from jax import lax
from jax.experimental import pallas as pl
from jax.experimental.pallas import tpu as pltpu
from jax.sharding import PartitionSpec as P

BF16 = jnp.bfloat16
F32 = jnp.float32
NY, NZ, NC = 2, 8, 2
NX, NW = 4, 2
HD = 128
BLK = 128
QPG = 4
ROWS = QPG * BLK
EMPTY = -1e30
SCALE2 = math.log2(math.e) / math.sqrt(HD)
OFFSETS = (0, 1, -1, 2, -2, 3, -3, 4)
NEAR = 5
STEPS = (1, 3, 0)
PAYLOAD = BLK + 16
PER_SOURCE = 12
KEYS_AT, VALUES_AT, MASK_AT = 0, PER_SOURCE * BLK, 2 * PER_SOURCE * BLK
SOURCE = MASK_AT + 16


def cache_step(x, dy, dz, dc):
    pairs = []
    for y in range(NY):
        for z in range(NZ):
            for c in range(NC):
                there = (((y + dy) % NY) * NZ + (z + dz) % NZ) * NC + (c + dc) % NC
                pairs.append(((y * NZ + z) * NC + c, there))
    return lax.ppermute(x, "cache", pairs)


def heads_step(x, dx, dw):
    pairs = []
    for a in range(NX):
        for w in range(NW):
            pairs.append((a * NW + w, ((a + dx) % NX) * NW + (w + dw) % NW))
    return lax.ppermute(x, "heads", pairs)


def z_ways(x, even, odd):
    pairs = []
    for y in range(NY):
        for z in range(NZ):
            for c in range(NC):
                there = (y * NZ + (z + (odd if z % 2 else even)) % NZ) * NC + c
                pairs.append(((y * NZ + z) * NC + c, there))
    return lax.ppermute(x, "cache", pairs)


def scores_of(keys, rows):
    return lax.dot_general(keys, rows, (((1,), (1,)), ((), ())), preferred_element_type=F32)


def weighted(values, weights):
    return lax.dot_general(
        values, weights.astype(BF16), (((0,), (0,)), ((), ())), preferred_element_type=F32
    )


def softmax_part(scores):
    peak = jnp.max(scores, axis=0, keepdims=True)
    weights = jnp.exp2((scores - peak) * SCALE2)
    return peak, jnp.sum(weights, axis=0, keepdims=True), weights


def fetch(packed, qbuf, qsem):
    copies = []
    for b, ref in enumerate(packed):
        for h in range(QPG):
            copies.append(
                pltpu.make_async_copy(
                    ref.at[pl.ds(0, BLK), pl.ds(h * HD, HD)],
                    qbuf.at[b, pl.ds(h * BLK, BLK), :],
                    qsem.at[b * QPG + h],
                )
            )
    for copy in copies:
        copy.start()
    return copies


def list_items(wanted, packed, sources, vis_v, vis_s, todo, dummy, vsem):
    blocks = sorted({b for b, _ in wanted})
    leaves = [packed[b][BLK:PAYLOAD, 0:HD].astype(F32)[0:1, :] for b in blocks]
    leaf = jnp.concatenate(leaves, axis=0)
    node_at = lax.broadcasted_iota(jnp.int32, leaf.shape, 1).astype(F32)
    chosen = jnp.where(node_at == leaf, 1.0, 0.0).astype(BF16)
    for s in sorted({s for _, s in wanted}):
        seen = scores_of(chosen, sources[s][MASK_AT:SOURCE, :])
        vis_v[8 * s : 8 * s + len(blocks), 0:16] = seen.astype(jnp.int32)
    copy = pltpu.make_async_copy(vis_v, vis_s, vsem)
    copy.start()
    copy.wait()
    count = jnp.int32(0)
    for b, s in wanted:
        for c in range(PER_SOURCE):
            todo[count] = b * 64 + s * 16 + c
            count = count + vis_s[8 * s + b, c]
    for i in range(6):
        todo[count + i] = dummy * 64
    return count


def work(count, todo, nq, qbuf, sources, state, ahead):
    def place(item):
        b = lax.shift_right_logical(item, 6)
        s = lax.bitwise_and(lax.shift_right_logical(item, 4), 3)
        return b, s, pl.multiple_of(lax.bitwise_and(item, 15) * BLK, BLK)

    def rows_of(s, row):
        rows = sources[0][pl.ds(row, BLK), :]
        for i in range(1, len(sources)):
            rows = jnp.where(s == i, sources[i][pl.ds(row, BLK), :], rows)
        return rows

    def scored(item):
        b, s, row = place(item)
        return scores_of(rows_of(s, row), qbuf[jnp.minimum(b, nq - 1)])

    def taken(item, scores):
        b, s, row = place(item)
        peak, total, weights = softmax_part(scores)
        return b, peak, total, weighted(rows_of(s, VALUES_AT + row), weights)

    def score_two(slot, at):
        ahead[slot, 0] = scored(todo[at])
        ahead[slot, 1] = scored(todo[at + 1])

    def take_two(slot, at):
        first = taken(todo[at], ahead[slot, 0])
        second = taken(todo[at + 1], ahead[slot, 1])
        merge(state, *first)
        merge(state, *second)

    def four(i, carry):
        score_two(1, 4 * i + 2)
        take_two(0, 4 * i)
        score_two(0, 4 * i + 4)
        take_two(1, 4 * i + 2)
        return carry

    score_two(0, 0)
    lax.fori_loop(0, lax.shift_right_logical(count + 3, 2), four, 0)


def merge(state, b, peak, total, summed):
    peaks, totals, sums = state
    before = peaks[b]
    after = jnp.maximum(before, peak)
    keep = jnp.exp2((before - after) * SCALE2)
    take = jnp.exp2((peak - after) * SCALE2)
    peaks[b] = after
    totals[b] = totals[b] * keep + total * take
    sums[b] = sums[b] * keep + summed * take


def column_copies(weight, out, sem, other_w, steps):
    x = lax.shift_right_logical(lax.axis_index("heads"), 1)
    w = lax.bitwise_xor(lax.bitwise_and(lax.axis_index("heads"), 1), other_w)
    width = out.shape[2]
    copies = []
    for j, dx in enumerate(steps):
        column = lax.bitwise_and(x + dx, NX - 1) * NW + w
        columns = pl.ds(pl.multiple_of(column * width, width), width)
        copies.append(pltpu.make_async_copy(weight.at[:, columns], out.at[j], sem.at[j]))
    for copy in copies:
        copy.start()
    return copies


def early_kernel(
    length, own, suffix_k, suffix_v, weight,
    peak, total, summed, far_w, home_w, piece, sem, home_sem, piece_sem,
):
    copies = column_copies(weight, far_w, sem, 1, STEPS)
    copies += column_copies(weight, home_w, home_sem, 0, STEPS[:-1])
    x = lax.shift_right_logical(lax.axis_index("heads"), 1)
    half, width = piece.shape
    part = weight.at[
        pl.ds(pl.multiple_of(lax.bitwise_and(lax.axis_index("cache"), 1) * half, half), half),
        pl.ds(pl.multiple_of(lax.bitwise_and(x + 2, NX - 1) * width, width), width),
    ]
    copies.append(pltpu.make_async_copy(part, piece, piece_sem))
    copies[-1].start()
    rows = jnp.concatenate([own[0:BLK, h * HD : (h + 1) * HD] for h in range(QPG)], axis=0)
    key_at = lax.broadcasted_iota(jnp.int32, (BLK, ROWS), 0)
    row_at = lax.bitwise_and(lax.broadcasted_iota(jnp.int32, (BLK, ROWS), 1), BLK - 1)
    scores = scores_of(suffix_k[...], rows)
    scores = jnp.where((key_at <= row_at) & (key_at < length[0]), scores, EMPTY)
    peak[...], total[...], weights = softmax_part(scores)
    summed[...] = weighted(suffix_v[...], weights)
    for copy in copies:
        copy.wait()


def laid_out(weight, steps):
    shape = (len(steps), weight.shape[0], weight.shape[1] // (NX * NW))
    return jax.ShapeDtypeStruct(shape, BF16)


def early(length, own, suffix_k, suffix_v, weight):
    return pl.pallas_call(
        early_kernel,
        out_shape=[
            jax.ShapeDtypeStruct((1, ROWS), F32),
            jax.ShapeDtypeStruct((1, ROWS), F32),
            jax.ShapeDtypeStruct((HD, ROWS), F32),
            laid_out(weight, STEPS),
            laid_out(weight, STEPS[:-1]),
            jax.ShapeDtypeStruct((weight.shape[0] // NC, weight.shape[1] // NX), BF16),
        ],
        in_specs=[SMEM] + [VMEM] * 3 + [HBM],
        out_specs=[VMEM] * 6,
        scratch_shapes=[
            pltpu.SemaphoreType.DMA((len(STEPS),)),
            pltpu.SemaphoreType.DMA((len(STEPS) - 1,)),
            pltpu.SemaphoreType.DMA,
        ],
        compiler_params=pltpu.CompilerParams(vmem_limit_bytes=46 << 20),
        cost_estimate=pl.CostEstimate(
            flops=40_000_000, bytes_accessed=9 << 20, transcendentals=70_000
        ),
        name="early",
    )(length, own, suffix_k, suffix_v, weight)


def late_kernel(steps, weight, home_w, sem):
    for copy in column_copies(weight, home_w, sem, 0, steps):
        copy.wait()


def late(name, weight, steps):
    return pl.pallas_call(
        functools.partial(late_kernel, steps),
        out_shape=laid_out(weight, steps),
        in_specs=[HBM],
        out_specs=VMEM,
        scratch_shapes=[pltpu.SemaphoreType.DMA((len(steps),))],
        compiler_params=pltpu.CompilerParams(vmem_limit_bytes=46 << 20),
        cost_estimate=pl.CostEstimate(flops=0, bytes_accessed=8 << 20, transcendentals=0),
        name=name,
    )(weight)


def first_kernel(*refs):
    packed, sources = refs[0:NEAR], refs[NEAR : NEAR + 2]
    suffix = refs[NEAR + 2 : NEAR + 5]
    state = refs[NEAR + 5 : NEAR + 8]
    todo, vis_s, vis_v, qbuf, ahead, qsem, vsem = refs[NEAR + 8 :]
    copies = fetch(packed, qbuf, qsem)
    wanted = [(b, s) for b in range(NEAR) for s in range(2)]
    count = list_items(wanted, packed, sources, vis_v, vis_s, todo, NEAR, vsem)
    peaks, totals, sums = state
    peaks[0], totals[0], sums[0] = suffix[0][...], suffix[1][...], suffix[2][...]
    clear(state, range(1, NEAR + 1))
    for copy in copies:
        copy.wait()
    work(count, todo, NEAR, qbuf, sources, state, ahead)


def clear(state, blocks):
    peaks, totals, sums = state
    for b in blocks:
        peaks[b] = jnp.full((1, ROWS), EMPTY, F32)
        totals[b] = jnp.zeros((1, ROWS), F32)
        sums[b] = jnp.zeros((HD, ROWS), F32)


def lse_rows(lse):
    high = lse.astype(BF16).astype(F32)
    middle = (lse - high).astype(BF16).astype(F32)
    low = lse - high - middle
    at = lax.broadcasted_iota(jnp.int32, (16, ROWS), 0)
    return jnp.where(at == 0, high, jnp.where(at == 1, middle, low)).astype(BF16)


def lse_of(rows):
    pieces = rows.astype(F32)
    return pieces[0:1] + pieces[1:2] + pieces[2:3]


def solve(wanted, packed, sources, scratch):
    todo, vis_s, vis_v, qbuf, ahead, peaks, totals, sums, qsem, vsem = scratch
    nq, state = len(packed), (peaks, totals, sums)
    copies = fetch(packed, qbuf, qsem)
    count = list_items(wanted, packed, sources, vis_v, vis_s, todo, nq, vsem)
    clear(state, range(nq + 1))
    for copy in copies:
        copy.wait()
    work(count, todo, nq, qbuf, sources, state, ahead)
    return state


def outcome(state, b):
    peaks, totals, sums = state
    total = totals[b]
    seen = total > 0.0
    safe = jnp.where(seen, total, 1.0)
    lse = jnp.where(seen, peaks[b] * SCALE2 + jnp.log2(safe), EMPTY)
    return sums[b] * (1.0 / safe), lse


def write_payload(state, b, ref):
    out, lse = outcome(state, b)
    ref[0:BLK, :] = out.astype(BF16)
    ref[BLK:PAYLOAD, :] = lse_rows(lse)


def far_kernel(*refs):
    packed, sources, state, scratch = refs[0:3], refs[3:6], refs[6:9], refs[9:]
    wanted = [(b, s) for b in range(3) for s in range(3)]
    solve(wanted, packed, sources, (*scratch[0:5], *state, *scratch[5:]))


def last_kernel(*refs):
    packed, sources, known, outs, scratch = refs[0:3], refs[3:4], refs[4:7], refs[7:10], refs[10:]
    state = solve([(b, 0) for b in range(3)], packed, sources, scratch)
    for b, ref in enumerate(outs):
        merge(state, b, known[0][b], known[1][b], known[2][b])
        write_payload(state, b, ref)


def near_kernel(*refs):
    packed, sources = refs[0:NEAR], refs[NEAR : NEAR + 2]
    known, outs = refs[NEAR + 2 : NEAR + 5], refs[NEAR + 5 : 2 * NEAR + 6]
    state = solve(
        [(b, s) for b in range(NEAR) for s in range(2)], packed, sources, refs[2 * NEAR + 6 :]
    )
    for b in range(NEAR):
        merge(state, b, known[0][b], known[1][b], known[2][b])
        if b == 0:
            out, lse = outcome(state, b)
            outs[0][...] = out
            outs[1][...] = jnp.broadcast_to(lse, outs[1].shape)
        else:
            write_payload(state, b, outs[b + 1])


SMEM = pl.BlockSpec(memory_space=pltpu.SMEM)
VMEM = pl.BlockSpec(memory_space=pltpu.VMEM)
HBM = pl.BlockSpec(memory_space=pltpu.HBM)


def state_shapes(count):
    return [(count, 1, ROWS), (count, 1, ROWS), (count, HD, ROWS)]


def buffers(nq):
    return [
        pltpu.SMEM((nq * 4 * PER_SOURCE + 8,), jnp.int32),
        pltpu.SMEM((32, HD), jnp.int32),
        pltpu.VMEM((32, HD), jnp.int32),
        pltpu.VMEM((nq, ROWS, HD), BF16),
        pltpu.VMEM((2, 2, BLK, ROWS), F32),
    ]


def semaphores(nq):
    return [pltpu.SemaphoreType.DMA((nq * QPG,)), pltpu.SemaphoreType.DMA]


def first_part(packed, sources, suffix):
    return pl.pallas_call(
        first_kernel,
        out_shape=[jax.ShapeDtypeStruct(s, F32) for s in state_shapes(NEAR + 1)],
        in_specs=[VMEM] * (NEAR + 5),
        out_specs=[VMEM] * 3,
        scratch_shapes=buffers(NEAR) + semaphores(NEAR),
        compiler_params=pltpu.CompilerParams(vmem_limit_bytes=12 << 20),
        cost_estimate=pl.CostEstimate(
            flops=2_000_000_000, bytes_accessed=4 << 20, transcendentals=1_000_000
        ),
        name="first_part",
    )(*packed, *sources, *suffix)


def solved(kernel, name, packed, sources, known, outs, flops, own_state):
    nq = len(packed)
    scratch = buffers(nq) + semaphores(nq)
    if own_state:
        scratch[5:5] = [pltpu.VMEM(s, F32) for s in state_shapes(nq + 1)]
    return pl.pallas_call(
        kernel,
        out_shape=outs,
        in_specs=[VMEM] * (nq + len(sources) + len(known)),
        out_specs=[VMEM] * len(outs),
        scratch_shapes=scratch,
        compiler_params=pltpu.CompilerParams(vmem_limit_bytes=14 << 20),
        cost_estimate=pl.CostEstimate(
            flops=flops, bytes_accessed=4 << 20, transcendentals=2_000_000
        ),
        name=name,
    )(*packed, *sources, *known)


def far_part(packed, sources):
    outs = [jax.ShapeDtypeStruct(s, F32) for s in state_shapes(len(packed) + 1)]
    return solved(far_kernel, "far_part", packed, sources, [], outs, 20_000_000_000, False)


def last_part(packed, sources, known):
    outs = [jax.ShapeDtypeStruct((PAYLOAD, ROWS), BF16)] * len(packed)
    return solved(last_kernel, "last_part", packed, sources, known, outs, 1_500_000_000, True)


def near_part(packed, sources, known):
    outs = [jax.ShapeDtypeStruct((HD, ROWS), F32), jax.ShapeDtypeStruct((8, ROWS), F32)]
    outs += [jax.ShapeDtypeStruct((PAYLOAD, ROWS), BF16)] * (len(packed) - 1)
    return solved(
        near_kernel, "near_part", packed, sources, known, outs, 2_500_000_000, True
    )


def join_kernel(ahead, back, from_ahead, from_back, from_far, ahead_out, back_out):
    odd = lax.bitwise_and(lax.shift_right_logical(lax.axis_index("cache"), 1), 1)
    for own, other, out, far_here in (
        (ahead, from_back, ahead_out, odd == 0),
        (back, from_ahead, back_out, odd == 1),
    ):
        parts = (own, other, from_far)
        lses = [lse_of(part[BLK:PAYLOAD, :]) for part in parts]
        lses[2] = jnp.where(far_here, lses[2], EMPTY)
        top = jnp.maximum(jnp.maximum(lses[0], lses[1]), lses[2])
        shares = [jnp.exp2(lse - top) for lse in lses]
        total = shares[0] + shares[1] + shares[2]
        inverse = 1.0 / total
        summed = parts[0][0:BLK, :].astype(F32) * (shares[0] * inverse)
        for part, share in zip(parts[1:], shares[1:]):
            summed = summed + part[0:BLK, :].astype(F32) * (share * inverse)
        out[0:BLK, :] = summed.astype(BF16)
        out[BLK:PAYLOAD, :] = lse_rows(jnp.maximum(top + jnp.log2(total), EMPTY))


def join(*parts):
    return pl.pallas_call(
        join_kernel,
        out_shape=[jax.ShapeDtypeStruct((PAYLOAD, ROWS), BF16)] * 2,
        in_specs=[VMEM] * 5,
        out_specs=[VMEM] * 2,
        compiler_params=pltpu.CompilerParams(vmem_limit_bytes=6 << 20),
        cost_estimate=pl.CostEstimate(
            flops=2_000_000, bytes_accessed=1 << 20, transcendentals=4096
        ),
        name="join",
    )(*parts)


def merged_rows(own_out, own_lse, payloads):
    lses = [own_lse[0:1, :]] + [lse_of(payload[BLK:PAYLOAD, :]) for payload in payloads]
    top = lses[0]
    for lse in lses[1:]:
        top = jnp.maximum(top, lse)
    parts_of = [jnp.exp2(lse - top) for lse in lses]
    total = parts_of[0]
    for part in parts_of[1:]:
        total = total + part
    inverse = 1.0 / total
    mixed = own_out[...] * (parts_of[0] * inverse)
    for payload, part in zip(payloads, parts_of[1:]):
        mixed = mixed + payload[0:BLK, :].astype(F32) * (part * inverse)
    return mixed


def project(rows, weights, outs):
    tile = 256
    for weight, out in zip(weights, outs):
        for t in range(weight.shape[1] // tile):
            columns = slice(t * tile, (t + 1) * tile)
            out[:, columns] = jnp.dot(
                rows, weight[:, columns], preferred_element_type=F32
            ).astype(out.dtype)


def away_kernel(own_out, own_lse, p1, m1, p2, m2, weight, rows_out, *outs):
    mixed = merged_rows(own_out, own_lse, (p1, m1, p2, m2))
    for h in range(QPG):
        columns = slice(h * BLK, (h + 1) * BLK)
        rows_out[:, columns] = mixed[:, columns].T.astype(BF16)
    project(rows_out[...], [weight.at[j] for j in range(len(outs))], outs)


def home_kernel(rows, weight, own_weight, *outs):
    weights = [weight.at[j] for j in range(len(outs) - 1)] + [own_weight.at[0]]
    project(rows[...], weights, outs)


def projected(kernel, name, operands, more):
    width = operands[-1].shape[2]
    return pl.pallas_call(
        kernel,
        out_shape=more
        + [jax.ShapeDtypeStruct((BLK, width), F32 if dx == 0 else BF16) for dx in STEPS],
        in_specs=[VMEM] * len(operands),
        out_specs=[VMEM] * (len(more) + len(STEPS)),
        compiler_params=pltpu.CompilerParams(vmem_limit_bytes=12 << 20),
        cost_estimate=pl.CostEstimate(
            flops=550_000_000, bytes_accessed=5 << 20, transcendentals=4096
        ),
        name=name,
    )(*operands)


def add_kernel(side, first, rows, mine, other, *refs):
    others, out = refs[:-1], refs[-1]
    core = lax.bitwise_and(lax.axis_index("cache"), 1)
    w = lax.bitwise_xor(lax.bitwise_and(lax.axis_index("heads"), 1), side)
    half, width = mine.shape[0], first.shape[1]
    low, high = rows[:, 0:half], rows[:, half:]
    left, right = jnp.where(core == 0, low, high), jnp.where(core == 0, high, low)
    tile = 256
    for t in range(width // tile):
        here = slice(t * tile, (t + 1) * tile)
        columns = pl.ds(pl.multiple_of(w * width + t * tile, tile), tile)
        total = first[:, here]
        for share in others:
            total = total + share[:, here].astype(F32)
        total = total + jnp.dot(left, mine[:, columns], preferred_element_type=F32)
        total = total + jnp.dot(right, other[:, columns], preferred_element_type=F32)
        out[:, here] = total.astype(out.dtype)


def add_two_away(name, side, dtype, first, rows, mine, other, others):
    return pl.pallas_call(
        functools.partial(add_kernel, side),
        out_shape=jax.ShapeDtypeStruct(first.shape, dtype),
        in_specs=[VMEM] * (4 + len(others)),
        out_specs=VMEM,
        compiler_params=pltpu.CompilerParams(vmem_limit_bytes=8 << 20),
        cost_estimate=pl.CostEstimate(
            flops=140_000_000, bytes_accessed=4 << 20, transcendentals=0
        ),
        name=name,
    )(first, rows, mine, other, *others)


def finish_kernel(first, *refs):
    others, out = refs[:-1], refs[-1]
    total = first[...]
    for other in others:
        total = total + other[...].astype(F32)
    out[...] = total.astype(out.dtype)


def finish(first, others):
    return pl.pallas_call(
        finish_kernel,
        out_shape=jax.ShapeDtypeStruct(first.shape, BF16),
        in_specs=[VMEM] * (1 + len(others)),
        out_specs=VMEM,
        compiler_params=pltpu.CompilerParams(vmem_limit_bytes=6 << 20),
        cost_estimate=pl.CostEstimate(
            flops=1_000_000, bytes_accessed=2 << 20, transcendentals=0
        ),
        name="finish",
    )(first, *others)


def shards(
    queries,
    cache_keys,
    cache_values,
    suffix_keys,
    suffix_values,
    out_weight,
    ancestor_mask,
    leaf_node,
    suffix_len,
):
    z = lax.bitwise_and(lax.shift_right_logical(lax.axis_index("cache"), 1), NZ - 1)
    leaf_rows = jnp.broadcast_to(leaf_node.astype(BF16)[:, None], (16, ROWS))
    own = jnp.concatenate([queries, leaf_rows], axis=0)
    count, nodes = ancestor_mask.shape[1], ancestor_mask.shape[0]
    mask = jnp.pad(ancestor_mask.T.astype(BF16), ((0, 16 - count), (0, HD - nodes)))
    source = jnp.concatenate([cache_keys, cache_values, mask], axis=0)
    across = cache_step(source, 1, 0, 0)
    p2, m2 = cache_step(own, 0, -2, 0), cache_step(own, 0, 2, 0)
    near = cache_step(source, 0, 0, 1)
    near, own = lax.optimization_barrier((near, own))
    p1, m1 = cache_step(own, 0, -1, 0), cache_step(own, 0, 1, 0)
    *suffix, far_w, home_w, piece = early(suffix_len, own, suffix_keys, suffix_values, out_weight)
    p2, m2, *suffix = lax.optimization_barrier((p2, m2, *suffix))
    mine = heads_step(piece, 2, 0)
    p3, m3 = cache_step(p2, 0, -1, 0), cache_step(m2, 0, 1, 0)
    p4 = z_ways(jnp.where(lax.bitwise_and(z, 1) == 0, m2, p2), 2, -2)
    known = first_part([own, p1, m1, p2, m2], [source, near], suffix)
    across, *known = lax.optimization_barrier((across, *known))
    far = cache_step(across, 0, 0, 1)
    far_known = far_part([p3, m3, p4], [source, near, across])
    o_p3, o_m3, o_p4 = last_part([p3, m3, p4], [far], far_known)
    from_far = z_ways(o_p4, 2, -2)
    from_back, from_ahead = cache_step(o_p3, 0, 1, 0), cache_step(o_m3, 0, -1, 0)
    o_p4, *known = lax.optimization_barrier((o_p4, *known))
    own_out, own_lse, o_p1, o_m1, o_p2, o_m2 = near_part(
        [own, p1, m1, p2, m2], [across, far], known
    )
    r_p1, r_m1 = cache_step(o_p1, 0, 1, 0), cache_step(o_m1, 0, -1, 0)
    near_weight, own_lse = lax.optimization_barrier((out_weight, own_lse))
    own_w = late("late_own", near_weight, STEPS[-1:])
    from_far, own_w = lax.optimization_barrier((from_far, own_w))
    ahead, back = join(o_p2, o_m2, from_ahead, from_back, from_far)
    r_p2, r_m2 = cache_step(ahead, 0, 2, 0), cache_step(back, 0, -2, 0)
    merged, *shares = projected(
        away_kernel,
        "away",
        [own_out, own_lse, r_p1, r_m1, r_p2, r_m2, far_w],
        [jax.ShapeDtypeStruct((BLK, ROWS), BF16)],
    )
    mine, _ = lax.optimization_barrier((mine, merged))
    two_away = heads_step(merged, 2, 0)
    arrived = [heads_step(share, dx, 0) for share, dx in zip(shares[:-1], STEPS)]
    other = cache_step(mine, 0, 0, 1)
    kept = projected(home_kernel, "home", [merged, home_w, own_w], [])
    passed = add_two_away("pass_on", 1, BF16, shares[-1], two_away, mine, other, arrived)
    passed = heads_step(passed, 0, 1)
    arrived = [heads_step(share, dx, 0) for share, dx in zip(kept[:-1], STEPS)]
    kept = add_two_away("keep", 0, F32, kept[-1], two_away, mine, other, [])
    return finish(kept, [*arrived, passed])


def solution(mesh):
    return jax.shard_map(
        shards,
        mesh=mesh,
        in_specs=(
            P("cache", "heads"),
            P("cache", "heads"),
            P("cache", "heads"),
            P("cache", "heads"),
            P("cache", "heads"),
            P("heads", None),
            P(None, "cache"),
            P("cache"),
            P("cache"),
        ),
        out_specs=P("cache", "heads"),
        check_vma=False,
    )
```

```python
import functools
import math

import jax
import jax.numpy as jnp
from jax import lax
from jax.experimental import pallas as pl
from jax.experimental.pallas import tpu as pltpu
from jax.sharding import PartitionSpec as P

BF16 = jnp.bfloat16
F32 = jnp.float32
NY, NZ, NC = 2, 8, 2
NX, NW = 4, 2
HD = 128
BLK = 128
QPG = 4
ROWS = QPG * BLK
EMPTY = -1e30
SCALE2 = math.log2(math.e) / math.sqrt(HD)
OFFSETS = (0, 1, -1, 2, -2, 3, -3, 4)
NEAR = 5
STEPS = (1, 3, 0)
PAYLOAD = BLK + 16
PER_SOURCE = 12
KEYS_AT, VALUES_AT, MASK_AT = 0, PER_SOURCE * BLK, 2 * PER_SOURCE * BLK
SOURCE = MASK_AT + 16


def cache_step(x, dy, dz, dc):
    pairs = []
    for y in range(NY):
        for z in range(NZ):
            for c in range(NC):
                there = (((y + dy) % NY) * NZ + (z + dz) % NZ) * NC + (c + dc) % NC
                pairs.append(((y * NZ + z) * NC + c, there))
    return lax.ppermute(x, "cache", pairs)


def heads_step(x, dx, dw):
    pairs = []
    for a in range(NX):
        for w in range(NW):
            pairs.append((a * NW + w, ((a + dx) % NX) * NW + (w + dw) % NW))
    return lax.ppermute(x, "heads", pairs)


def z_ways(x, even, odd):
    pairs = []
    for y in range(NY):
        for z in range(NZ):
            for c in range(NC):
                there = (y * NZ + (z + (odd if z % 2 else even)) % NZ) * NC + c
                pairs.append(((y * NZ + z) * NC + c, there))
    return lax.ppermute(x, "cache", pairs)


def scores_of(keys, rows):
    return lax.dot_general(keys, rows, (((1,), (1,)), ((), ())), preferred_element_type=F32)


def weighted(values, weights):
    return lax.dot_general(
        values, weights.astype(BF16), (((0,), (0,)), ((), ())), preferred_element_type=F32
    )


def softmax_part(scores):
    peak = jnp.max(scores, axis=0, keepdims=True)
    weights = jnp.exp2((scores - peak) * SCALE2)
    return peak, jnp.sum(weights, axis=0, keepdims=True), weights


def fetch(packed, qbuf, qsem):
    copies = []
    for b, ref in enumerate(packed):
        for h in range(QPG):
            copies.append(
                pltpu.make_async_copy(
                    ref.at[pl.ds(0, BLK), pl.ds(h * HD, HD)],
                    qbuf.at[b, pl.ds(h * BLK, BLK), :],
                    qsem.at[b * QPG + h],
                )
            )
    for copy in copies:
        copy.start()
    return copies


def list_items(wanted, packed, sources, vis_v, vis_s, todo, dummy, vsem):
    blocks = sorted({b for b, _ in wanted})
    leaves = [packed[b][BLK:PAYLOAD, 0:HD].astype(F32)[0:1, :] for b in blocks]
    leaf = jnp.concatenate(leaves, axis=0)
    node_at = lax.broadcasted_iota(jnp.int32, leaf.shape, 1).astype(F32)
    chosen = jnp.where(node_at == leaf, 1.0, 0.0).astype(BF16)
    for s in sorted({s for _, s in wanted}):
        seen = scores_of(chosen, sources[s][MASK_AT:SOURCE, :])
        vis_v[8 * s : 8 * s + len(blocks), 0:16] = seen.astype(jnp.int32)
    copy = pltpu.make_async_copy(vis_v, vis_s, vsem)
    copy.start()
    copy.wait()
    count = jnp.int32(0)
    for b, s in wanted:
        for c in range(PER_SOURCE):
            todo[count] = b * 64 + s * 16 + c
            count = count + vis_s[8 * s + b, c]
    for i in range(6):
        todo[count + i] = dummy * 64
    return count


def work(count, todo, nq, qbuf, sources, state, ahead):
    def place(item):
        b = lax.shift_right_logical(item, 6)
        s = lax.bitwise_and(lax.shift_right_logical(item, 4), 3)
        return b, s, pl.multiple_of(lax.bitwise_and(item, 15) * BLK, BLK)

    def rows_of(s, row):
        rows = sources[0][pl.ds(row, BLK), :]
        for i in range(1, len(sources)):
            rows = jnp.where(s == i, sources[i][pl.ds(row, BLK), :], rows)
        return rows

    def scored(item):
        b, s, row = place(item)
        return scores_of(rows_of(s, row), qbuf[jnp.minimum(b, nq - 1)])

    def taken(item, scores):
        b, s, row = place(item)
        peak, total, weights = softmax_part(scores)
        return b, peak, total, weighted(rows_of(s, VALUES_AT + row), weights)

    def score_two(slot, at):
        ahead[slot, 0] = scored(todo[at])
        ahead[slot, 1] = scored(todo[at + 1])

    def take_two(slot, at):
        first = taken(todo[at], ahead[slot, 0])
        second = taken(todo[at + 1], ahead[slot, 1])
        merge(state, *first)
        merge(state, *second)

    def four(i, carry):
        score_two(1, 4 * i + 2)
        take_two(0, 4 * i)
        score_two(0, 4 * i + 4)
        take_two(1, 4 * i + 2)
        return carry

    score_two(0, 0)
    lax.fori_loop(0, lax.shift_right_logical(count + 3, 2), four, 0)


def merge(state, b, peak, total, summed):
    peaks, totals, sums = state
    before = peaks[b]
    after = jnp.maximum(before, peak)
    keep = jnp.exp2((before - after) * SCALE2)
    take = jnp.exp2((peak - after) * SCALE2)
    peaks[b] = after
    totals[b] = totals[b] * keep + total * take
    sums[b] = sums[b] * keep + summed * take


def column_copies(weight, out, sem, other_w, steps):
    x = lax.shift_right_logical(lax.axis_index("heads"), 1)
    w = lax.bitwise_xor(lax.bitwise_and(lax.axis_index("heads"), 1), other_w)
    width = out.shape[2]
    copies = []
    for j, dx in enumerate(steps):
        column = lax.bitwise_and(x + dx, NX - 1) * NW + w
        columns = pl.ds(pl.multiple_of(column * width, width), width)
        copies.append(pltpu.make_async_copy(weight.at[:, columns], out.at[j], sem.at[j]))
    for copy in copies:
        copy.start()
    return copies


def early_kernel(
    length, own, suffix_k, suffix_v, weight,
    peak, total, summed, far_w, home_w, piece, sem, home_sem, piece_sem,
):
    copies = column_copies(weight, far_w, sem, 1, STEPS)
    copies += column_copies(weight, home_w, home_sem, 0, STEPS)
    x = lax.shift_right_logical(lax.axis_index("heads"), 1)
    half, width = piece.shape
    part = weight.at[
        pl.ds(pl.multiple_of(lax.bitwise_and(lax.axis_index("cache"), 1) * half, half), half),
        pl.ds(pl.multiple_of(lax.bitwise_and(x + 2, NX - 1) * width, width), width),
    ]
    copies.append(pltpu.make_async_copy(part, piece, piece_sem))
    copies[-1].start()
    rows = jnp.concatenate([own[0:BLK, h * HD : (h + 1) * HD] for h in range(QPG)], axis=0)
    key_at = lax.broadcasted_iota(jnp.int32, (BLK, ROWS), 0)
    row_at = lax.bitwise_and(lax.broadcasted_iota(jnp.int32, (BLK, ROWS), 1), BLK - 1)
    scores = scores_of(suffix_k[...], rows)
    scores = jnp.where((key_at <= row_at) & (key_at < length[0]), scores, EMPTY)
    peak[...], total[...], weights = softmax_part(scores)
    summed[...] = weighted(suffix_v[...], weights)
    for copy in copies:
        copy.wait()


def laid_out(weight, steps):
    shape = (len(steps), weight.shape[0], weight.shape[1] // (NX * NW))
    return jax.ShapeDtypeStruct(shape, BF16)


def early(length, own, suffix_k, suffix_v, weight):
    return pl.pallas_call(
        early_kernel,
        out_shape=[
            jax.ShapeDtypeStruct((1, ROWS), F32),
            jax.ShapeDtypeStruct((1, ROWS), F32),
            jax.ShapeDtypeStruct((HD, ROWS), F32),
            laid_out(weight, STEPS),
            laid_out(weight, STEPS),
            jax.ShapeDtypeStruct((weight.shape[0] // NC, weight.shape[1] // NX), BF16),
        ],
        in_specs=[SMEM] + [VMEM] * 3 + [HBM],
        out_specs=[VMEM] * 6,
        scratch_shapes=[
            pltpu.SemaphoreType.DMA((len(STEPS),)),
            pltpu.SemaphoreType.DMA((len(STEPS),)),
            pltpu.SemaphoreType.DMA,
        ],
        compiler_params=pltpu.CompilerParams(vmem_limit_bytes=46 << 20),
        cost_estimate=pl.CostEstimate(
            flops=40_000_000, bytes_accessed=9 << 20, transcendentals=70_000
        ),
        name="early",
    )(length, own, suffix_k, suffix_v, weight)


def first_kernel(*refs):
    packed, sources = refs[0:NEAR], refs[NEAR : NEAR + 2]
    suffix = refs[NEAR + 2 : NEAR + 5]
    state = refs[NEAR + 5 : NEAR + 8]
    todo, vis_s, vis_v, qbuf, ahead, qsem, vsem = refs[NEAR + 8 :]
    copies = fetch(packed, qbuf, qsem)
    wanted = [(b, s) for b in range(NEAR) for s in range(2)]
    count = list_items(wanted, packed, sources, vis_v, vis_s, todo, NEAR, vsem)
    peaks, totals, sums = state
    peaks[0], totals[0], sums[0] = suffix[0][...], suffix[1][...], suffix[2][...]
    clear(state, range(1, NEAR + 1))
    for copy in copies:
        copy.wait()
    work(count, todo, NEAR, qbuf, sources, state, ahead)


def clear(state, blocks):
    peaks, totals, sums = state
    for b in blocks:
        peaks[b] = jnp.full((1, ROWS), EMPTY, F32)
        totals[b] = jnp.zeros((1, ROWS), F32)
        sums[b] = jnp.zeros((HD, ROWS), F32)


def lse_rows(lse):
    high = lse.astype(BF16).astype(F32)
    middle = (lse - high).astype(BF16).astype(F32)
    low = lse - high - middle
    at = lax.broadcasted_iota(jnp.int32, (16, ROWS), 0)
    return jnp.where(at == 0, high, jnp.where(at == 1, middle, low)).astype(BF16)


def lse_of(rows):
    pieces = rows.astype(F32)
    return pieces[0:1] + pieces[1:2] + pieces[2:3]


def solve(wanted, packed, sources, scratch):
    todo, vis_s, vis_v, qbuf, ahead, peaks, totals, sums, qsem, vsem = scratch
    nq, state = len(packed), (peaks, totals, sums)
    copies = fetch(packed, qbuf, qsem)
    count = list_items(wanted, packed, sources, vis_v, vis_s, todo, nq, vsem)
    clear(state, range(nq + 1))
    for copy in copies:
        copy.wait()
    work(count, todo, nq, qbuf, sources, state, ahead)
    return state


def outcome(state, b):
    peaks, totals, sums = state
    total = totals[b]
    seen = total > 0.0
    safe = jnp.where(seen, total, 1.0)
    lse = jnp.where(seen, peaks[b] * SCALE2 + jnp.log2(safe), EMPTY)
    return sums[b] * (1.0 / safe), lse


def write_payload(state, b, ref):
    out, lse = outcome(state, b)
    ref[0:BLK, :] = out.astype(BF16)
    ref[BLK:PAYLOAD, :] = lse_rows(lse)


def far_kernel(*refs):
    packed, sources, state, scratch = refs[0:3], refs[3:6], refs[6:9], refs[9:]
    wanted = [(b, s) for b in range(3) for s in range(3)]
    solve(wanted, packed, sources, (*scratch[0:5], *state, *scratch[5:]))


def last_kernel(*refs):
    packed, sources, known, outs, scratch = refs[0:3], refs[3:4], refs[4:7], refs[7:10], refs[10:]
    state = solve([(b, 0) for b in range(3)], packed, sources, scratch)
    for b, ref in enumerate(outs):
        merge(state, b, known[0][b], known[1][b], known[2][b])
        write_payload(state, b, ref)


def near_kernel(*refs):
    packed, sources = refs[0:NEAR], refs[NEAR : NEAR + 2]
    known, outs = refs[NEAR + 2 : NEAR + 5], refs[NEAR + 5 : 2 * NEAR + 6]
    state = solve(
        [(b, s) for b in range(NEAR) for s in range(2)], packed, sources, refs[2 * NEAR + 6 :]
    )
    for b in range(NEAR):
        merge(state, b, known[0][b], known[1][b], known[2][b])
        if b == 0:
            out, lse = outcome(state, b)
            outs[0][...] = out
            outs[1][...] = jnp.broadcast_to(lse, outs[1].shape)
        else:
            write_payload(state, b, outs[b + 1])


SMEM = pl.BlockSpec(memory_space=pltpu.SMEM)
VMEM = pl.BlockSpec(memory_space=pltpu.VMEM)
HBM = pl.BlockSpec(memory_space=pltpu.HBM)


def state_shapes(count):
    return [(count, 1, ROWS), (count, 1, ROWS), (count, HD, ROWS)]


def buffers(nq):
    return [
        pltpu.SMEM((nq * 4 * PER_SOURCE + 8,), jnp.int32),
        pltpu.SMEM((32, HD), jnp.int32),
        pltpu.VMEM((32, HD), jnp.int32),
        pltpu.VMEM((nq, ROWS, HD), BF16),
        pltpu.VMEM((2, 2, BLK, ROWS), F32),
    ]


def semaphores(nq):
    return [pltpu.SemaphoreType.DMA((nq * QPG,)), pltpu.SemaphoreType.DMA]


def first_part(packed, sources, suffix):
    return pl.pallas_call(
        first_kernel,
        out_shape=[jax.ShapeDtypeStruct(s, F32) for s in state_shapes(NEAR + 1)],
        in_specs=[VMEM] * (NEAR + 5),
        out_specs=[VMEM] * 3,
        scratch_shapes=buffers(NEAR) + semaphores(NEAR),
        compiler_params=pltpu.CompilerParams(vmem_limit_bytes=12 << 20),
        cost_estimate=pl.CostEstimate(
            flops=2_000_000_000, bytes_accessed=4 << 20, transcendentals=1_000_000
        ),
        name="first_part",
    )(*packed, *sources, *suffix)


def solved(kernel, name, packed, sources, known, outs, flops, own_state):
    nq = len(packed)
    scratch = buffers(nq) + semaphores(nq)
    if own_state:
        scratch[5:5] = [pltpu.VMEM(s, F32) for s in state_shapes(nq + 1)]
    return pl.pallas_call(
        kernel,
        out_shape=outs,
        in_specs=[VMEM] * (nq + len(sources) + len(known)),
        out_specs=[VMEM] * len(outs),
        scratch_shapes=scratch,
        compiler_params=pltpu.CompilerParams(vmem_limit_bytes=14 << 20),
        cost_estimate=pl.CostEstimate(
            flops=flops, bytes_accessed=4 << 20, transcendentals=2_000_000
        ),
        name=name,
    )(*packed, *sources, *known)


def far_part(packed, sources):
    outs = [jax.ShapeDtypeStruct(s, F32) for s in state_shapes(len(packed) + 1)]
    return solved(far_kernel, "far_part", packed, sources, [], outs, 20_000_000_000, False)


def last_part(packed, sources, known):
    outs = [jax.ShapeDtypeStruct((PAYLOAD, ROWS), BF16)] * len(packed)
    return solved(last_kernel, "last_part", packed, sources, known, outs, 1_500_000_000, True)


def near_part(packed, sources, known):
    outs = [jax.ShapeDtypeStruct((HD, ROWS), F32), jax.ShapeDtypeStruct((8, ROWS), F32)]
    outs += [jax.ShapeDtypeStruct((PAYLOAD, ROWS), BF16)] * (len(packed) - 1)
    return solved(
        near_kernel, "near_part", packed, sources, known, outs, 2_500_000_000, True
    )


def join_kernel(ahead, back, from_ahead, from_back, from_far, ahead_out, back_out):
    odd = lax.bitwise_and(lax.shift_right_logical(lax.axis_index("cache"), 1), 1)
    for own, other, out, far_here in (
        (ahead, from_back, ahead_out, odd == 0),
        (back, from_ahead, back_out, odd == 1),
    ):
        parts = (own, other, from_far)
        lses = [lse_of(part[BLK:PAYLOAD, :]) for part in parts]
        lses[2] = jnp.where(far_here, lses[2], EMPTY)
        top = jnp.maximum(jnp.maximum(lses[0], lses[1]), lses[2])
        shares = [jnp.exp2(lse - top) for lse in lses]
        total = shares[0] + shares[1] + shares[2]
        inverse = 1.0 / total
        summed = parts[0][0:BLK, :].astype(F32) * (shares[0] * inverse)
        for part, share in zip(parts[1:], shares[1:]):
            summed = summed + part[0:BLK, :].astype(F32) * (share * inverse)
        out[0:BLK, :] = summed.astype(BF16)
        out[BLK:PAYLOAD, :] = lse_rows(jnp.maximum(top + jnp.log2(total), EMPTY))


def join(*parts):
    return pl.pallas_call(
        join_kernel,
        out_shape=[jax.ShapeDtypeStruct((PAYLOAD, ROWS), BF16)] * 2,
        in_specs=[VMEM] * 5,
        out_specs=[VMEM] * 2,
        compiler_params=pltpu.CompilerParams(vmem_limit_bytes=6 << 20),
        cost_estimate=pl.CostEstimate(
            flops=2_000_000, bytes_accessed=1 << 20, transcendentals=4096
        ),
        name="join",
    )(*parts)


def merged_rows(own_out, own_lse, payloads):
    lses = [own_lse[0:1, :]] + [lse_of(payload[BLK:PAYLOAD, :]) for payload in payloads]
    top = lses[0]
    for lse in lses[1:]:
        top = jnp.maximum(top, lse)
    parts_of = [jnp.exp2(lse - top) for lse in lses]
    total = parts_of[0]
    for part in parts_of[1:]:
        total = total + part
    inverse = 1.0 / total
    mixed = own_out[...] * (parts_of[0] * inverse)
    for payload, part in zip(payloads, parts_of[1:]):
        mixed = mixed + payload[0:BLK, :].astype(F32) * (part * inverse)
    return mixed


def project(rows, weights, outs):
    tile = 256
    for weight, out in zip(weights, outs):
        for t in range(weight.shape[1] // tile):
            columns = slice(t * tile, (t + 1) * tile)
            out[:, columns] = jnp.dot(
                rows, weight[:, columns], preferred_element_type=F32
            ).astype(out.dtype)


def merge_kernel(own_out, own_lse, p1, m1, p2, m2, rows_out):
    mixed = merged_rows(own_out, own_lse, (p1, m1, p2, m2))
    for h in range(QPG):
        columns = slice(h * BLK, (h + 1) * BLK)
        rows_out[:, columns] = mixed[:, columns].T.astype(BF16)


def merge_all(*operands):
    return pl.pallas_call(
        merge_kernel,
        out_shape=jax.ShapeDtypeStruct((BLK, ROWS), BF16),
        in_specs=[VMEM] * len(operands),
        out_specs=VMEM,
        compiler_params=pltpu.CompilerParams(vmem_limit_bytes=8 << 20),
        cost_estimate=pl.CostEstimate(
            flops=2_000_000, bytes_accessed=1 << 20, transcendentals=4096
        ),
        name="merge_all",
    )(*operands)


def share_kernel(rows, weight, *outs):
    project(rows[...], [weight.at[j] for j in range(len(outs))], outs)


def projected(kernel, name, operands):
    width = operands[-1].shape[2]
    return pl.pallas_call(
        kernel,
        out_shape=[
            jax.ShapeDtypeStruct((BLK, width), F32 if dx == 0 else BF16) for dx in STEPS
        ],
        in_specs=[VMEM] * len(operands),
        out_specs=[VMEM] * len(STEPS),
        compiler_params=pltpu.CompilerParams(vmem_limit_bytes=12 << 20),
        cost_estimate=pl.CostEstimate(
            flops=550_000_000, bytes_accessed=5 << 20, transcendentals=4096
        ),
        name=name,
    )(*operands)


def two_share_kernel(rows, mine, other, away, home, away_out, home_out):
    core = lax.bitwise_and(lax.axis_index("cache"), 1)
    w = lax.bitwise_and(lax.axis_index("heads"), 1)
    half, width = mine.shape[0], away.shape[1]
    low, high = rows[:, 0:half], rows[:, half:]
    left, right = jnp.where(core == 0, low, high), jnp.where(core == 0, high, low)
    tile = 256
    for first, out, side in ((away, away_out, 1 - w), (home, home_out, w)):
        for t in range(width // tile):
            here = slice(t * tile, (t + 1) * tile)
            columns = pl.ds(pl.multiple_of(side * width + t * tile, tile), tile)
            total = jnp.dot(left, mine[:, columns], preferred_element_type=F32)
            total = total + jnp.dot(right, other[:, columns], preferred_element_type=F32)
            out[:, here] = total + first[:, here]


def add_two_away(*operands):
    shape = jax.ShapeDtypeStruct(operands[-1].shape, F32)
    return pl.pallas_call(
        two_share_kernel,
        out_shape=[shape, shape],
        in_specs=[VMEM] * len(operands),
        out_specs=[VMEM] * 2,
        compiler_params=pltpu.CompilerParams(vmem_limit_bytes=8 << 20),
        cost_estimate=pl.CostEstimate(
            flops=20_000_000_000, bytes_accessed=4 << 20, transcendentals=0
        ),
        name="add_two_away",
    )(*operands)


def finish_kernel(first, *refs):
    others, out = refs[:-1], refs[-1]
    total = first[...]
    for other in others:
        total = total + other[...].astype(F32)
    out[...] = total.astype(out.dtype)


def finish(name, first, others):
    return pl.pallas_call(
        finish_kernel,
        out_shape=jax.ShapeDtypeStruct(first.shape, BF16),
        in_specs=[VMEM] * (1 + len(others)),
        out_specs=VMEM,
        compiler_params=pltpu.CompilerParams(vmem_limit_bytes=6 << 20),
        cost_estimate=pl.CostEstimate(
            flops=1_000_000, bytes_accessed=2 << 20, transcendentals=0
        ),
        name=name,
    )(first, *others)


def shards(
    queries,
    cache_keys,
    cache_values,
    suffix_keys,
    suffix_values,
    out_weight,
    ancestor_mask,
    leaf_node,
    suffix_len,
):
    z = lax.bitwise_and(lax.shift_right_logical(lax.axis_index("cache"), 1), NZ - 1)
    leaf_rows = jnp.broadcast_to(leaf_node.astype(BF16)[:, None], (16, ROWS))
    own = jnp.concatenate([queries, leaf_rows], axis=0)
    count, nodes = ancestor_mask.shape[1], ancestor_mask.shape[0]
    mask = jnp.pad(ancestor_mask.T.astype(BF16), ((0, 16 - count), (0, HD - nodes)))
    source = jnp.concatenate([cache_keys, cache_values, mask], axis=0)
    across = cache_step(source, 1, 0, 0)
    p2, m2 = cache_step(own, 0, -2, 0), cache_step(own, 0, 2, 0)
    near = cache_step(source, 0, 0, 1)
    near, own = lax.optimization_barrier((near, own))
    p1, m1 = cache_step(own, 0, -1, 0), cache_step(own, 0, 1, 0)
    *suffix, far_w, home_w, piece = early(suffix_len, own, suffix_keys, suffix_values, out_weight)
    p2, m2, *suffix = lax.optimization_barrier((p2, m2, *suffix))
    mine = heads_step(piece, 2, 0)
    p3, m3 = cache_step(p2, 0, -1, 0), cache_step(m2, 0, 1, 0)
    p4 = z_ways(jnp.where(lax.bitwise_and(z, 1) == 0, m2, p2), 2, -2)
    known = first_part([own, p1, m1, p2, m2], [source, near], suffix)
    across, *known = lax.optimization_barrier((across, *known))
    far = cache_step(across, 0, 0, 1)
    far_known = far_part([p3, m3, p4], [source, near, across])
    o_p3, o_m3, o_p4 = last_part([p3, m3, p4], [far], far_known)
    from_far = z_ways(o_p4, 2, -2)
    from_back, from_ahead = cache_step(o_p3, 0, 1, 0), cache_step(o_m3, 0, -1, 0)
    o_p4, *known = lax.optimization_barrier((o_p4, *known))
    own_out, own_lse, o_p1, o_m1, o_p2, o_m2 = near_part(
        [own, p1, m1, p2, m2], [across, far], known
    )
    r_p1, r_m1 = cache_step(o_p1, 0, 1, 0), cache_step(o_m1, 0, -1, 0)
    ahead, back = join(o_p2, o_m2, from_ahead, from_back, from_far)
    r_p2, r_m2 = cache_step(ahead, 0, 2, 0), cache_step(back, 0, -2, 0)
    merged = merge_all(own_out, own_lse, r_p1, r_m1, r_p2, r_m2)
    shares = projected(share_kernel, "away", [merged, far_w])
    mine, _ = lax.optimization_barrier((mine, merged))
    two_away = heads_step(merged, 2, 0)
    arrived = [heads_step(share, dx, 0) for share, dx in zip(shares[:-1], STEPS)]
    other = cache_step(mine, 0, 0, 1)
    kept = projected(share_kernel, "home", [merged, home_w])
    away, home = add_two_away(two_away, mine, other, shares[-1], kept[-1])
    away, *kept = lax.optimization_barrier((away, *kept))
    passed = heads_step(finish("pass_on", away, arrived), 0, 1)
    arrived = [heads_step(share, dx, 0) for share, dx in zip(kept[:-1], STEPS)]
    return finish("finish", home, [*arrived, passed])


def solution(mesh):
    return jax.shard_map(
        shards,
        mesh=mesh,
        in_specs=(
            P("cache", "heads"),
            P("cache", "heads"),
            P("cache", "heads"),
            P("cache", "heads"),
            P("cache", "heads"),
            P("heads", None),
            P(None, "cache"),
            P("cache"),
            P("cache"),
        ),
        out_specs=P("cache", "heads"),
        check_vma=False,
    )
```
